32 devices in a mesh: lon: 8 (over z, core), lat: 4 (over y, x).
Axes of the slice: x: 2, y: 2, z: 4, core: 2. Of those that a mesh axis runs over, the one named last changes fastest.
Arguments:
- tokens: bfloat16 [2, 48, 96, 192], P(None, 'lat', 'lon'), may hold values from -6 to 6
- cotangent: bfloat16 [2, 48, 96, 192], P(None, 'lat', 'lon'), may hold values from -6 to 6
- qkv_codes: int32 [192, 576], replicated, may hold values from -128 to 127
- proj_codes: int32 [192, 192], replicated, may hold values from -128 to 127
- up_codes: int32 [192, 768], replicated, may hold values from -128 to 127
- down_codes: int32 [768, 192], replicated, may hold values from -128 to 127
- bit_widths: int32 [4], replicated, may hold values from 6 to 8
- quant_scales: int32 [4], replicated, may hold values from 300 to 599
- bias_table: bfloat16 [8, 1, 6, 3312], P('lat'), may hold values from -4 to 302
- bias_index: int32 [20736], replicated, may hold values from 0 to 3311
- merge_weight: bfloat16 [768, 384], replicated, may hold values from -0.21875 to 0.21875
Outputs:
- merged: bfloat16 [2, 24, 48, 384], P(None, 'lat', 'lon')
- grad_tokens: bfloat16 [2, 48, 96, 192], P(None, 'lat', 'lon')
- grad_qkv: bfloat16 [192, 576], replicated
- grad_proj: bfloat16 [192, 192], replicated
- grad_up: bfloat16 [192, 768], replicated
- grad_down: bfloat16 [768, 192], replicated
The draws below stay inside these ranges and needn't reach their ends.
All inputs are finite; a program needn't handle non-finite values.
Results may differ from the reference program's by a relative error of at most 0.024.
The reference program's roundings to bfloat16 on the way count: a program that leaves them out, or rounds other values in their place, can miss the bound.
Values may be sent and summed in bfloat16 or wider, within the bound.
A program may use at most 128 MiB of HBM per device.

```python
import math
import jax
import jax.numpy as jnp
from jax import lax

C = 192
HEADS = 6
FF = 768
HEAD_DIM = 32
LEV = 2
WLEV = 2
WLAT = 6
WLON = 12
ROWS_DEV = 12
WTOK = 144
POS = 3312
LATT = 48
LATS = 37
LONT = 96
BIAS_ROWS = 8
N_LAT = 4


def draw_bias_table(key, part):
    key = jax.random.fold_in(key, 7)
    key_base = jax.random.fold_in(key, 0)
    table_shape = (BIAS_ROWS, LEV // WLEV, HEADS, POS)
    values = jnp.clip(jax.random.normal(key_base, table_shape, jnp.float32), -4.0, 4.0)
    return values.astype(jnp.bfloat16)


def set_ends(result, own_key, smallest, high):
    index_at = [jax.random.randint(jax.random.fold_in(own_key, axis), (), 0, length) for axis, length in enumerate(result.shape)]
    widest = result.shape.index(max(result.shape))
    beside = index_at[:widest] + [(index_at[widest] + 1) % result.shape[widest]] + index_at[widest + 1:]
    return result.at[tuple(index_at)].set(smallest).at[tuple(beside)].set(high)


def block_scale(stream_key, shape, shards, smallest, top_value):
    def one(dim, blocks):
        heights = jax.random.uniform(jax.random.fold_in(jax.random.fold_in(stream_key, 6), dim), (blocks,), jnp.float32, smallest / len(shards), top_value / len(shards))
        return jnp.repeat(jnp.exp(heights), shape[dim] // blocks).reshape((-1,) + (1,) * (len(shape) - dim - 1))

    level = one(*shards[0])
    for cut in shards[1:]:
        level = level * one(*cut)
    return level


def normal_values(stream_key, extent, deviation, reach, cuts=(), kind=jnp.bfloat16):
    array = jax.random.normal(stream_key, extent, jnp.float32) * deviation
    if len(cuts) > 0:
        array = block_scale(stream_key, extent, cuts, -0.22, 0.18) * array
    return jnp.clip(array, min=-reach, max=reach).astype(kind)


def setup_inputs(seed: int = 0) -> dict:
    key_of = jax.random.split(jax.random.key(seed), 12)
    return {
        "tokens": normal_values(key_of[0], (LEV, LATT, LONT, C), 1.0, 6.0, ((1, 4), (2, 8))),
        "cotangent": normal_values(key_of[1], (LEV, LATT, LONT, C), 1.0, 6.0, ((1, 4), (2, 8))),
        "qkv_codes": set_ends(jax.random.randint(key_of[2], (C, 3 * C), -128, 128), jax.random.fold_in(key_of[2], 1), -128, 127).astype(jnp.int32),
        "proj_codes": set_ends(jax.random.randint(key_of[3], (C, C), -128, 128), jax.random.fold_in(key_of[3], 1), -128, 127).astype(jnp.int32),
        "up_codes": set_ends(jax.random.randint(key_of[4], (C, FF), -128, 128), jax.random.fold_in(key_of[4], 1), -128, 127).astype(jnp.int32),
        "down_codes": set_ends(jax.random.randint(key_of[5], (FF, C), -128, 128), jax.random.fold_in(key_of[5], 1), -128, 127).astype(jnp.int32),
        "bit_widths": set_ends(jax.random.randint(key_of[6], (4,), 6, 9), jax.random.fold_in(key_of[6], 1), 6, 8).astype(jnp.int32),
        "quant_scales": set_ends(jax.random.randint(key_of[7], (4,), 300, 600), jax.random.fold_in(key_of[7], 1), 300, 599).astype(jnp.int32),
        "bias_table": draw_bias_table(jax.random.fold_in(key_of[11], 71), 0),
        "bias_index": set_ends(jax.random.randint(key_of[9], (WTOK * WTOK,), 0, POS), jax.random.fold_in(key_of[9], 1), 0, POS - 1).astype(jnp.int32),
        "merge_weight": normal_values(key_of[10], (4 * C, 2 * C), (4 * C) ** -0.5, 0.21875),
    }


EPSILON = 1e-05
MASKED = -1000000000.0

def product(left, right):
    return jnp.dot(left, right, preferred_element_type=jnp.float32)

def crossed(left, right):
    return jnp.dot(left.T, right, preferred_element_type=jnp.float32)

def dequant(int_codes, bit_count, quant_scale, fan_in):
    largest = jnp.left_shift(jnp.ones((), jnp.int32), bit_count - 1) - 1
    clipped = jnp.clip(int_codes, -largest, largest).astype(jnp.float32)
    factor = math.sqrt(C / fan_in) / quant_scale.astype(jnp.float32)
    return (clipped * factor).astype(jnp.bfloat16)

def normalize(values):
    center = values - lax.optimization_barrier(jnp.mean(values, axis=-1, keepdims=True))
    spread = lax.optimization_barrier(jnp.mean(center * center, axis=-1, keepdims=True))
    return center * lax.rsqrt(spread + EPSILON)

def norm_back(source, upstream):
    pullback = jax.vjp(normalize, source.astype(jnp.float32))[1]
    return pullback(upstream.astype(jnp.float32))[0]

def gelu_back(pre_act, upstream):
    pullback = jax.vjp(jax.nn.gelu, pre_act)[1]
    return pullback(upstream.astype(jnp.float32))[0]

def allowed_table(lat_start, lat_limit, level_count, row_windows):
    position = jnp.arange(WTOK, dtype=jnp.int32)
    level_in = position // (WLAT * WLON)
    row_in = position // WLON % WLAT
    window_level = WLEV * jnp.arange(level_count // WLEV, dtype=jnp.int32)
    levels = (window_level[:, None] + level_in[None, :] + 1) % level_count
    group = (levels + 1) // 2
    same = group[:, :, None] == group[:, None, :]
    lat_rows = lat_start + WLAT * jnp.arange(row_windows, dtype=jnp.int32)[:, None] + row_in[None, :]
    key_ok = (lat_rows >= 0) & (lat_rows < lat_limit)
    allowed = same[:, None, :, :] & key_ok[None, :, None, :]
    return allowed.reshape(-1, WTOK, WTOK)

def window_terms(table_rows, bias_index, lat_start, lat_limit, level_count):
    row_windows = table_rows.shape[0]
    level_windows = level_count // WLEV
    gathered = table_rows[:, :, :, bias_index].astype(jnp.float32)
    gathered = gathered.reshape(row_windows, level_windows, HEADS, WTOK, WTOK).transpose(1, 0, 2, 3, 4)
    gathered = gathered.reshape(level_windows * row_windows, HEADS, WTOK, WTOK)
    return (gathered, allowed_table(lat_start, lat_limit, level_count, row_windows))

def to_windows(window_frame):
    level_count, row_count, col_count, feat_count = window_frame.shape
    rolled = jnp.roll(window_frame, -1, axis=0)
    pieces = rolled.reshape(level_count // WLEV, WLEV, row_count // WLAT, WLAT, col_count // WLON, WLON, feat_count)
    return pieces.transpose(0, 2, 4, 1, 3, 5, 6).reshape(-1, WTOK, feat_count)

def from_windows(windows, level_count, row_count, col_count):
    feat_count = windows.shape[-1]
    pieces = windows.reshape(level_count // WLEV, row_count // WLAT, col_count // WLON, WLEV, WLAT, WLON, feat_count)
    pieces = pieces.transpose(0, 3, 1, 4, 2, 5, 6).reshape(level_count, row_count, col_count, feat_count)
    return jnp.roll(pieces, 1, axis=0)

def attend(windows, bias_terms, allowed):
    window_count = windows.shape[0]
    group_count = bias_terms.shape[0]
    query_part, key_part, value_part = jnp.split(windows.astype(jnp.float32), 3, axis=-1)
    query_part = query_part.reshape(window_count, WTOK, HEADS, HEAD_DIM)
    key_part = key_part.reshape(window_count, WTOK, HEADS, HEAD_DIM)
    value_part = value_part.reshape(window_count, WTOK, HEADS, HEAD_DIM)
    scores = jnp.einsum('wqhd,wkhd->whqk', query_part, key_part) * HEAD_DIM ** (-0.5)
    scores = scores.reshape(group_count, window_count // group_count, HEADS, WTOK, WTOK) + bias_terms[:, None]
    scores = jnp.where(allowed[:, None, None], scores, MASKED)
    top_score = lax.optimization_barrier(jnp.max(scores, axis=-1, keepdims=True))
    weights = jnp.exp(scores - top_score)
    weights = (weights / lax.optimization_barrier(jnp.sum(weights, axis=-1, keepdims=True))).astype(jnp.bfloat16)
    weights = weights.reshape(window_count, HEADS, WTOK, WTOK)
    mixed = jnp.einsum('whqk,wkhd->wqhd', weights.astype(jnp.float32), value_part)
    return mixed.reshape(window_count, WTOK, C)

def merge_patches(final, merge_weight):
    level_count, row_count, col_count, feat_count = final.shape
    grouped = final.reshape(level_count, row_count // 2, 2, col_count // 2, 2, feat_count)
    grouped = grouped.transpose(0, 1, 3, 2, 4, 5).reshape(-1, 4 * feat_count)
    normed = normalize(grouped.astype(jnp.float32)).astype(jnp.bfloat16)
    merged = product(normed, merge_weight).astype(jnp.bfloat16)
    return merged.reshape(level_count, row_count // 2, col_count // 2, 2 * feat_count)

def shift_in(source):
    blank = jnp.zeros_like(source[:, :WLAT // 2])
    moved = jnp.concatenate([blank, source[:, :-(WLAT // 2)]], axis=1)
    return jnp.roll(moved, WLON // 2, axis=2)

def shift_out(source):
    moved = jnp.roll(source, -(WLON // 2), axis=2)
    blank = jnp.zeros_like(moved[:, :WLAT // 2])
    return jnp.concatenate([moved[:, WLAT // 2:], blank], axis=1)

def to_frames(source):
    return source.reshape(LEV, N_LAT, ROWS_DEV, LONT, -1).transpose(1, 0, 2, 3, 4)

def from_frames(stack):
    return stack.transpose(1, 0, 2, 3, 4).reshape(LEV, LATT, LONT, -1)

def reference(tokens, cotangent, qkv_codes, proj_codes, up_codes, down_codes, bit_widths, quant_scales, bias_table, bias_index, merge_weight):
    w_qkv = dequant(qkv_codes, bit_widths[0], quant_scales[0], C)
    w_proj = dequant(proj_codes, bit_widths[1], quant_scales[1], C)
    w_up = dequant(up_codes, bit_widths[2], quant_scales[2], C)
    w_down = dequant(down_codes, bit_widths[3], quant_scales[3], FF)
    token_count = LEV * LATT * LONT
    row_mask = (jnp.arange(LATT, dtype=jnp.int32) < LATS)[None, :, None, None]
    start = jnp.where(row_mask, tokens, jnp.zeros_like(tokens))
    start_flat = start.reshape(token_count, C)
    normed = normalize(start_flat.astype(jnp.float32)).astype(jnp.bfloat16)
    qkv = product(normed, w_qkv).astype(jnp.bfloat16).reshape(LEV, LATT, LONT, 3 * C)
    lat_ids = jnp.arange(N_LAT, dtype=jnp.int32)
    table_frames = bias_table.reshape(N_LAT, ROWS_DEV // WLAT, LEV // WLEV, HEADS, POS)

    def forward_frame(payload):
        frame_qkv, table_rows, lat_id = payload
        bias_terms, allowed = window_terms(table_rows, bias_index, lat_id * ROWS_DEV - WLAT // 2, LATS, LEV)
        outcome = attend(to_windows(frame_qkv), bias_terms, allowed)
        return from_windows(outcome.astype(jnp.bfloat16), LEV, ROWS_DEV, LONT)
    heads_out = shift_out(from_frames(lax.map(forward_frame, (to_frames(shift_in(qkv)), table_frames, lat_ids))))
    heads_flat = heads_out.reshape(token_count, C)
    resid = (start_flat.astype(jnp.float32) + product(heads_flat, w_proj)).astype(jnp.bfloat16)
    normed_two = normalize(resid.astype(jnp.float32)).astype(jnp.bfloat16)
    pre_act = product(normed_two, w_up)
    hidden = jax.nn.gelu(pre_act).astype(jnp.bfloat16)
    final = (resid.astype(jnp.float32) + product(hidden, w_down)).reshape(LEV, LATT, LONT, C)
    final = jnp.where(row_mask, final, 0.0).astype(jnp.bfloat16)
    merged = merge_patches(final, merge_weight)
    d_out = jnp.where(row_mask, cotangent, jnp.zeros_like(cotangent)).reshape(token_count, C)
    down_total = crossed(hidden, d_out)
    d_hidden = product(d_out, w_down.T).astype(jnp.bfloat16)
    d_pre = gelu_back(pre_act, d_hidden).astype(jnp.bfloat16)
    up_total = crossed(normed_two, d_pre)
    d_normed_two = product(d_pre, w_up.T).astype(jnp.bfloat16)
    d_resid = (d_out.astype(jnp.float32) + norm_back(resid, d_normed_two)).astype(jnp.bfloat16)
    proj_total = crossed(heads_flat, d_resid)
    d_heads = product(d_resid, w_proj.T).astype(jnp.bfloat16).reshape(LEV, LATT, LONT, C)

    def backward_frame(payload):
        frame_qkv, frame_grad, table_rows, lat_id = payload
        bias_terms, allowed = window_terms(table_rows, bias_index, lat_id * ROWS_DEV - WLAT // 2, LATS, LEV)

        def local_attend(windows):
            return attend(windows, bias_terms, allowed)
        pullback = jax.vjp(local_attend, to_windows(frame_qkv))[1]
        upstream = to_windows(frame_grad).astype(jnp.float32)
        return from_windows(pullback(upstream)[0], LEV, ROWS_DEV, LONT)
    stacked = lax.map(backward_frame, (to_frames(shift_in(qkv)), to_frames(shift_in(d_heads)), table_frames, lat_ids))
    d_qkv = shift_out(from_frames(stacked)).reshape(token_count, 3 * C)
    qkv_total = crossed(normed, d_qkv)
    d_normed = product(d_qkv, w_qkv.T).astype(jnp.bfloat16)
    grad_flat = d_resid.astype(jnp.float32) + norm_back(start_flat, d_normed)
    grad_tokens = jnp.where(row_mask, grad_flat.reshape(LEV, LATT, LONT, C), 0.0).astype(jnp.bfloat16)
    return (merged, grad_tokens, qkv_total.astype(jnp.bfloat16), proj_total.astype(jnp.bfloat16), up_total.astype(jnp.bfloat16), down_total.astype(jnp.bfloat16))
```

```python
import functools
import math

import jax
import jax.numpy as jnp
from jax import lax
from jax.experimental import pallas as pl
from jax.experimental.pallas import tpu as pltpu
from jax.sharding import PartitionSpec as P

C = 192
HEADS = 6
FF = 768
HEAD_DIM = 32
WLAT = 6
WLON = 12
LAT_PAD = 11
WTOK = 144
HALF = 72
LANES = 128
EPSILON = 1e-05
MASKED = -1000000000.0
F32 = jnp.float32
BF16 = jnp.bfloat16


def shifted(block, axis, by, wrap):
    count = lax.axis_size(axis)
    route = [(i, (i + by) % count) for i in range(count) if wrap or 0 <= i + by < count]
    return lax.ppermute(block, axis, route)


def pull_rim(source):
    lat_part = shifted(source[:, -(WLAT // 2) :], "lat", 1, False)
    upper = jnp.concatenate([lat_part, source[:, : -(WLAT // 2)]], axis=1)
    lon_part = shifted(upper[:, :, -(WLON // 2) :], "lon", 1, True)
    return jnp.concatenate([lon_part, upper[:, :, : -(WLON // 2)]], axis=2)


def push_rim(frame):
    lon_part = shifted(frame[:, :, : WLON // 2], "lon", -1, True)
    upper = jnp.concatenate([frame[:, :, WLON // 2 :], lon_part], axis=2)
    lat_part = shifted(upper[:, : WLAT // 2], "lat", -1, False)
    return jnp.concatenate([upper[:, WLAT // 2 :], lat_part], axis=1)


def nn(left, right):
    return lax.dot_general(left, right, (((1,), (0,)), ((), ())), preferred_element_type=F32)


def nt(left, right):
    return lax.dot_general(left, right, (((1,), (1,)), ((), ())), preferred_element_type=F32)


def tn(left, right):
    return lax.dot_general(left, right, (((0,), (0,)), ((), ())), preferred_element_type=F32)


def gather_kernel(pieces, index_ref, table_ref, out_ref):
    index = index_ref[...]
    low = jnp.bitwise_and(index, LANES - 1)
    high = jnp.right_shift(index, 7)

    def one_row(r, carry):
        total = jnp.zeros(index.shape, F32)
        for piece in range(pieces):
            source = jnp.broadcast_to(table_ref[r, pl.ds(piece, 1), :], index.shape)
            found = jnp.take_along_axis(source, low, axis=1, mode="promise_in_bounds")
            total = jnp.where(high == piece, found, total)
        out_ref[r] = total
        return carry

    lax.fori_loop(0, table_ref.shape[0], one_row, 0)


def center_of(values):
    center = values - jnp.mean(values, axis=-1, keepdims=True)
    spread = jnp.mean(center * center, axis=-1, keepdims=True)
    return center, lax.rsqrt(spread + EPSILON)


def norm_back(center, scale, upstream):
    inner = jnp.mean(upstream * center, axis=-1, keepdims=True)
    outer = jnp.mean(upstream, axis=-1, keepdims=True)
    return scale * (upstream - outer - center * (scale * scale * inner))


def block_kernel(
    window_rows,
    edges_ref,
    bits_ref,
    scales_ref,
    start_ref,
    d_out_ref,
    qkv_ref,
    proj_ref,
    up_ref,
    down_ref,
    bias_ref,
    final_ref,
    grad_ref,
    qkv_total_ref,
    proj_total_ref,
    up_total_ref,
    down_total_ref,
    heads_s,
    dq_s,
    dk_s,
    dv_s,
):
    def dequant(codes, layer, fan_in):
        largest = jnp.left_shift(jnp.int32(1), bits_ref[layer] - 1) - 1
        scale = jnp.full((1, codes.shape[1]), scales_ref[layer].astype(F32), F32)
        factor = math.sqrt(C / fan_in) / scale
        return (jnp.clip(codes, -largest, largest).astype(F32) * factor).astype(BF16)

    w_q = dequant(qkv_ref[:, :C], 0, C)
    w_k = dequant(qkv_ref[:, C : 2 * C], 0, C)
    w_v = dequant(qkv_ref[:, 2 * C :], 0, C)
    w_proj = dequant(proj_ref[...], 1, C)
    start = start_ref[...].astype(F32)
    center, inverse = center_of(start)
    normed = (center * inverse).astype(BF16)
    q = nn(normed, w_q).astype(BF16)
    k = nn(normed, w_k).astype(BF16)
    v = nn(normed, w_v).astype(BF16)

    lane = lax.broadcasted_iota(jnp.int32, (HALF, C), 1)
    head_masks = [(lane >= h * HEAD_DIM) & (lane < (h + 1) * HEAD_DIM) for h in range(HEADS)]

    def stack(values):
        wide = values.astype(F32)
        return jnp.concatenate([jnp.where(m, wide, 0.0) for m in head_masks], axis=0).astype(BF16)

    def unstack(values):
        total = jnp.zeros((HALF, C), F32)
        for h, m in enumerate(head_masks):
            total = jnp.where(m, values[h * HALF : (h + 1) * HALF], total)
        return total

    keys = lax.broadcasted_iota(jnp.int32, (HEADS * HALF, HALF), 1)
    blocks = start.shape[0] // HALF
    saved = []
    for b in range(blocks):
        level, a = b // window_rows, b % window_rows
        part = slice(b * HALF, (b + 1) * HALF)
        stacked_q = stack(q[part])
        bias = bias_ref[a * HEADS : (a + 1) * HEADS, (1 - level) * HALF : (2 - level) * HALF, :]
        bias = bias.reshape(HEADS * HALF, LANES)[:, :HALF]
        scores = nt(stacked_q, k[part]) * HEAD_DIM ** (-0.5) + bias
        allowed = (keys >= edges_ref[2 * a]) & (keys < edges_ref[2 * a + 1])
        scores = jnp.where(allowed, scores, MASKED)
        weights = jnp.exp(scores - jnp.max(scores, axis=-1, keepdims=True))
        weights = weights / jnp.sum(weights, axis=-1, keepdims=True)
        saved.append((stacked_q, weights, allowed))
        heads_s[part, :] = unstack(nn(weights.astype(BF16), v[part]))

    heads = heads_s[...].astype(BF16)
    resid = (start + nn(heads, w_proj)).astype(BF16)
    center_two, inverse_two = center_of(resid.astype(F32))
    normed_two = (center_two * inverse_two).astype(BF16)
    w_up = dequant(up_ref[...], 2, C)
    w_down = dequant(down_ref[...], 3, FF)
    pre = nn(normed_two, w_up)
    cubic = math.sqrt(2 / math.pi)
    square = pre * pre
    bent = jnp.tanh(cubic * (pre + 0.044715 * square * pre))
    hidden = (0.5 * pre * (1.0 + bent)).astype(BF16)
    final_ref[...] = (resid.astype(F32) + nn(hidden, w_down)).astype(BF16)
    d_out = d_out_ref[...]
    down_total_ref[...] = tn(hidden, d_out).astype(BF16)
    d_hidden = nt(d_out, w_down).astype(BF16).astype(F32)
    slope = 0.5 * (1.0 + bent) + 0.5 * pre * (1.0 - bent * bent) * cubic * (
        1.0 + 3 * 0.044715 * square
    )
    d_pre = (slope * d_hidden).astype(BF16)
    up_total_ref[...] = tn(normed_two, d_pre).astype(BF16)
    d_normed_two = nt(d_pre, w_up).astype(BF16).astype(F32)
    d_resid = (d_out.astype(F32) + norm_back(center_two, inverse_two, d_normed_two)).astype(BF16)
    proj_total_ref[...] = tn(heads, d_resid).astype(BF16)
    d_heads = nt(d_resid, w_proj).astype(BF16)

    for b in range(blocks):
        part = slice(b * HALF, (b + 1) * HALF)
        stacked_q, weights, allowed = saved[b]
        d_stacked = stack(d_heads[part])
        d_weights = nt(d_stacked, v[part]).astype(BF16).astype(F32)
        dv_s[part, :] = tn(weights.astype(BF16), d_stacked)
        inner = jnp.sum(weights * d_weights, axis=-1, keepdims=True)
        d_scores = jnp.where(allowed, weights * (d_weights - inner), 0.0)
        d_scores = (d_scores * HEAD_DIM ** (-0.5)).astype(BF16)
        dq_s[part, :] = unstack(nn(d_scores, k[part]))
        dk_s[part, :] = tn(d_scores, stacked_q)

    dq = dq_s[...].astype(BF16)
    dk = dk_s[...].astype(BF16)
    dv = dv_s[...].astype(BF16)
    qkv_total_ref[:, :C] = tn(normed, dq).astype(BF16)
    qkv_total_ref[:, C : 2 * C] = tn(normed, dk).astype(BF16)
    qkv_total_ref[:, 2 * C :] = tn(normed, dv).astype(BF16)
    d_normed = (nt(dq, w_q) + nt(dk, w_k) + nt(dv, w_v)).astype(BF16).astype(F32)
    grad_ref[...] = (d_resid.astype(F32) + norm_back(center, inverse, d_normed)).astype(BF16)


def merge_patches(final, merge_weight):
    level_count, row_count, col_count, feat_count = final.shape
    grouped = final.reshape(level_count, row_count // 2, 2, col_count // 2, 2, feat_count)
    grouped = grouped.transpose(0, 1, 3, 2, 4, 5).reshape(-1, 4 * feat_count)
    center, inverse = center_of(grouped.astype(F32))
    merged = nn((center * inverse).astype(BF16), merge_weight).astype(BF16)
    return merged.reshape(level_count, row_count // 2, col_count // 2, 2 * feat_count)


def per_device(
    tokens,
    cotangent,
    qkv_codes,
    proj_codes,
    up_codes,
    down_codes,
    bit_widths,
    quant_scales,
    bias_table,
    bias_index,
    merge_weight,
):
    level_count, row_count, col_count, feat_count = tokens.shape
    token_count = level_count * row_count * col_count
    window_rows = row_count // WLAT
    grid_shape = (level_count, row_count, col_count)
    lat_limit = lax.axis_size("lat") * row_count - LAT_PAD
    lat_index = lax.axis_index("lat")
    lat_start = lat_index * row_count - WLAT // 2
    row_ids = lat_index * row_count + jnp.arange(row_count, dtype=jnp.int32)
    row_mask = (row_ids < lat_limit)[None, :, None, None]

    both = jnp.concatenate([tokens, cotangent], axis=-1)
    both = jnp.where(row_mask, both, jnp.zeros_like(both))
    frame = pull_rim(both).reshape(token_count, 2 * feat_count)

    pair = bias_index.reshape(2, HALF, 2, HALF)
    index = jnp.concatenate([pair[0, :, 0], pair[1, :, 1]], axis=0)
    index = jnp.pad(index, ((0, 0), (0, LANES - HALF)))
    positions = bias_table.shape[-1]
    pieces = -(-positions // LANES)
    table = bias_table.reshape(window_rows * HEADS, positions).astype(F32)
    table = jnp.pad(table, ((0, 0), (0, pieces * LANES - positions)))
    table = table.reshape(window_rows * HEADS, pieces, LANES)
    vmem = pl.BlockSpec(memory_space=pltpu.VMEM)
    smem = pl.BlockSpec(memory_space=pltpu.SMEM)
    bias = pl.pallas_call(
        functools.partial(gather_kernel, pieces),
        out_shape=jax.ShapeDtypeStruct((window_rows * HEADS, WTOK, LANES), F32),
        in_specs=[vmem, vmem],
        out_specs=vmem,
        compiler_params=pltpu.CompilerParams(vmem_limit_bytes=32 * 2**20),
        cost_estimate=pl.CostEstimate(flops=10**9, bytes_accessed=4 * 10**6, transcendentals=0),
        name="bias_gather",
    )(index, table)

    first_row = lat_start + WLAT * jnp.arange(window_rows, dtype=jnp.int32)
    edges = jnp.stack([-first_row * WLON, (lat_limit - first_row) * WLON], axis=1).reshape(-1)
    wide = jax.ShapeDtypeStruct((token_count, feat_count), BF16)
    final, grad, qkv_total, proj_total, up_total, down_total = pl.pallas_call(
        functools.partial(block_kernel, window_rows),
        out_shape=[
            wide,
            wide,
            jax.ShapeDtypeStruct((C, 3 * C), BF16),
            jax.ShapeDtypeStruct((C, C), BF16),
            jax.ShapeDtypeStruct((C, FF), BF16),
            jax.ShapeDtypeStruct((FF, C), BF16),
        ],
        in_specs=[smem] * 3 + [vmem] * 7,
        out_specs=[vmem] * 6,
        scratch_shapes=[pltpu.VMEM((token_count, feat_count), F32)] * 4,
        compiler_params=pltpu.CompilerParams(vmem_limit_bytes=48 * 2**20),
        name="block",
    )(
        edges,
        bit_widths,
        quant_scales,
        frame[:, :feat_count],
        frame[:, feat_count:],
        qkv_codes,
        proj_codes,
        up_codes,
        down_codes,
        bias,
    )
    summed = lax.psum((qkv_total, proj_total, up_total, down_total), ("lon", "lat"))
    owned = push_rim(jnp.concatenate([final, grad], axis=-1).reshape(grid_shape + (-1,)))
    owned = jnp.where(row_mask, owned, jnp.zeros_like(owned))
    merged = merge_patches(owned[..., :feat_count], merge_weight)
    return (merged, owned[..., feat_count:]) + tuple(summed)


def solution(mesh):
    split = P(None, "lat", "lon", None)
    placed = (split, split, P(), P(), P(), P(), P(), P(), P("lat", None, None, None), P(), P())
    return jax.shard_map(
        per_device,
        mesh=mesh,
        in_specs=placed,
        out_specs=(split, split, P(), P(), P(), P()),
        check_vma=False,
    )
```

```python
import functools
import math

import jax
import jax.numpy as jnp
from jax import lax
from jax.experimental import pallas as pl
from jax.experimental.pallas import tpu as pltpu
from jax.sharding import PartitionSpec as P

C = 192
HEADS = 6
FF = 768
HEAD_DIM = 32
WLAT = 6
WLON = 12
LAT_PAD = 11
WTOK = 144
HALF = 72
LANES = 128
EPSILON = 1e-05
MASKED = -1000000000.0
UP_AT = 6 * C
DOWN_AT = 12 * C
PAIR_AT = 16 * C
TOTAL_ROWS = 18 * C
F32 = jnp.float32
BF16 = jnp.bfloat16


def shifted(block, axis, by, wrap):
    count = lax.axis_size(axis)
    route = [(i, (i + by) % count) for i in range(count) if wrap or 0 <= i + by < count]
    return lax.ppermute(block, axis, route)


def pull_rim(source):
    lat_part = shifted(source[:, -(WLAT // 2) :], "lat", 1, False)
    upper = jnp.concatenate([lat_part, source[:, : -(WLAT // 2)]], axis=1)
    lon_part = shifted(upper[:, :, -(WLON // 2) :], "lon", 1, True)
    return jnp.concatenate([lon_part, upper[:, :, : -(WLON // 2)]], axis=2)


def nn(left, right):
    return lax.dot_general(left, right, (((1,), (0,)), ((), ())), preferred_element_type=F32)


def nt(left, right):
    return lax.dot_general(left, right, (((1,), (1,)), ((), ())), preferred_element_type=F32)


def tn(left, right):
    return lax.dot_general(left, right, (((0,), (0,)), ((), ())), preferred_element_type=F32)


def gather_kernel(pieces, index_ref, table_ref, out_ref):
    index = index_ref[...]
    low = jnp.bitwise_and(index, LANES - 1)
    high = jnp.right_shift(index, 7)

    def one_row(r, carry):
        total = jnp.zeros(index.shape, F32)
        for piece in range(pieces):
            source = jnp.broadcast_to(table_ref[r, pl.ds(piece, 1), :], index.shape)
            found = jnp.take_along_axis(source, low, axis=1, mode="promise_in_bounds")
            total = jnp.where(high == piece, found, total)
        out_ref[r] = total
        return carry

    lax.fori_loop(0, table_ref.shape[0], one_row, 0)


def center_of(values):
    center = values - jnp.mean(values, axis=-1, keepdims=True)
    spread = jnp.mean(center * center, axis=-1, keepdims=True)
    return center, lax.rsqrt(spread + EPSILON)


def norm_back(center, scale, upstream):
    inner = jnp.mean(upstream * center, axis=-1, keepdims=True)
    outer = jnp.mean(upstream, axis=-1, keepdims=True)
    return scale * (upstream - outer - center * (scale * scale * inner))


def block_kernel(
    window_rows,
    edges_ref,
    bits_ref,
    scales_ref,
    start_ref,
    d_out_ref,
    qkv_ref,
    proj_ref,
    up_ref,
    down_ref,
    bias_ref,
    final_ref,
    grad_ref,
    totals_ref,
    heads_s,
    dq_s,
    dk_s,
    dv_s,
    narrow_s,
    pair_s,
):
    def dequant(codes, layer, fan_in):
        largest = jnp.left_shift(jnp.int32(1), bits_ref[layer] - 1) - 1
        scale = jnp.full((1, codes.shape[1]), scales_ref[layer].astype(F32), F32)
        factor = math.sqrt(C / fan_in) / scale
        return (jnp.clip(codes, -largest, largest).astype(F32) * factor).astype(BF16)

    w_q = dequant(qkv_ref[:, :C], 0, C)
    w_k = dequant(qkv_ref[:, C : 2 * C], 0, C)
    w_v = dequant(qkv_ref[:, 2 * C :], 0, C)
    w_proj = dequant(proj_ref[...], 1, C)
    start = start_ref[...].astype(F32)
    center, inverse = center_of(start)
    normed = (center * inverse).astype(BF16)
    q = nn(normed, w_q).astype(BF16)
    k = nn(normed, w_k).astype(BF16)
    v = nn(normed, w_v).astype(BF16)

    lane = lax.broadcasted_iota(jnp.int32, (HALF, C), 1)
    head_masks = [(lane >= h * HEAD_DIM) & (lane < (h + 1) * HEAD_DIM) for h in range(HEADS)]

    def stack(values):
        wide = values.astype(F32)
        return jnp.concatenate([jnp.where(m, wide, 0.0) for m in head_masks], axis=0).astype(BF16)

    def unstack(values):
        total = jnp.zeros((HALF, C), F32)
        for h, m in enumerate(head_masks):
            total = jnp.where(m, values[h * HALF : (h + 1) * HALF], total)
        return total

    keys = lax.broadcasted_iota(jnp.int32, (HEADS * HALF, HALF), 1)
    blocks = start.shape[0] // HALF
    saved = []
    for b in range(blocks):
        level, a = b // window_rows, b % window_rows
        part = slice(b * HALF, (b + 1) * HALF)
        stacked_q = stack(q[part])
        bias = bias_ref[a * HEADS : (a + 1) * HEADS, (1 - level) * HALF : (2 - level) * HALF, :]
        bias = bias.reshape(HEADS * HALF, LANES)[:, :HALF]
        scores = nt(stacked_q, k[part]) * HEAD_DIM ** (-0.5) + bias
        allowed = (keys >= edges_ref[2 * a]) & (keys < edges_ref[2 * a + 1])
        scores = jnp.where(allowed, scores, MASKED)
        weights = jnp.exp(scores - jnp.max(scores, axis=-1, keepdims=True))
        weights = weights / jnp.sum(weights, axis=-1, keepdims=True)
        saved.append((stacked_q, weights, allowed))
        heads_s[part, :] = unstack(nn(weights.astype(BF16), v[part]))

    heads = heads_s[...].astype(BF16)
    resid = (start + nn(heads, w_proj)).astype(BF16)
    center_two, inverse_two = center_of(resid.astype(F32))
    normed_two = (center_two * inverse_two).astype(BF16)
    w_up = dequant(up_ref[...], 2, C)
    w_down = dequant(down_ref[...], 3, FF)
    pre = nn(normed_two, w_up)
    cubic = math.sqrt(2 / math.pi)
    square = pre * pre
    bent = jnp.tanh(cubic * (pre + 0.044715 * square * pre))
    hidden = (0.5 * pre * (1.0 + bent)).astype(BF16)
    final_ref[...] = (resid.astype(F32) + nn(hidden, w_down)).astype(BF16)
    d_out = d_out_ref[...]
    down_total = tn(hidden, d_out)
    totals_ref[DOWN_AT : DOWN_AT + FF, :] = down_total[:, :LANES].astype(BF16)
    pair_s[:, : C - LANES] = down_total[: FF // 2, LANES:]
    pair_s[:, C - LANES :] = down_total[FF // 2 :, LANES:]
    totals_ref[PAIR_AT : PAIR_AT + FF // 2, :] = pair_s[...].astype(BF16)
    d_hidden = nt(d_out, w_down).astype(BF16).astype(F32)
    slope = 0.5 * (1.0 + bent) + 0.5 * pre * (1.0 - bent * bent) * cubic * (
        1.0 + 3 * 0.044715 * square
    )
    d_pre = (slope * d_hidden).astype(BF16)
    up_total = tn(normed_two, d_pre).astype(BF16)
    for t in range(FF // LANES):
        totals_ref[UP_AT + t * C : UP_AT + (t + 1) * C, :] = up_total[:, t * LANES : (t + 1) * LANES]
    d_normed_two = nt(d_pre, w_up).astype(BF16).astype(F32)
    d_resid = (d_out.astype(F32) + norm_back(center_two, inverse_two, d_normed_two)).astype(BF16)
    narrow_s[:, 3 * C :] = tn(heads, d_resid)
    d_heads = nt(d_resid, w_proj).astype(BF16)

    for b in range(blocks):
        part = slice(b * HALF, (b + 1) * HALF)
        stacked_q, weights, allowed = saved[b]
        d_stacked = stack(d_heads[part])
        d_weights = nt(d_stacked, v[part]).astype(BF16).astype(F32)
        dv_s[part, :] = tn(weights.astype(BF16), d_stacked)
        inner = jnp.sum(weights * d_weights, axis=-1, keepdims=True)
        d_scores = jnp.where(allowed, weights * (d_weights - inner), 0.0)
        d_scores = (d_scores * HEAD_DIM ** (-0.5)).astype(BF16)
        dq_s[part, :] = unstack(nn(d_scores, k[part]))
        dk_s[part, :] = tn(d_scores, stacked_q)

    dq = dq_s[...].astype(BF16)
    dk = dk_s[...].astype(BF16)
    dv = dv_s[...].astype(BF16)
    narrow_s[:, :C] = tn(normed, dq)
    narrow_s[:, C : 2 * C] = tn(normed, dk)
    narrow_s[:, 2 * C : 3 * C] = tn(normed, dv)
    for t in range(4 * C // LANES):
        tile = narrow_s[:, t * LANES : (t + 1) * LANES]
        totals_ref[t * C : (t + 1) * C, :] = tile.astype(BF16)
    spare = totals_ref.shape[0] - TOTAL_ROWS
    if spare:
        totals_ref[TOTAL_ROWS:, :] = jnp.zeros((spare, LANES), BF16)
    d_normed = (nt(dq, w_q) + nt(dk, w_k) + nt(dv, w_v)).astype(BF16).astype(F32)
    grad_ref[...] = (d_resid.astype(F32) + norm_back(center, inverse, d_normed)).astype(BF16)


def reduce_kernel(
    lon_count,
    lat_count,
    rim_parts,
    totals_ref,
    rim_ref,
    grad_qkv_ref,
    grad_proj_ref,
    grad_up_ref,
    grad_down_ref,
    rim_out_ref,
    core_in,
    lat_in,
    far_in,
    half_s,
    part_s,
    result,
    rim_in,
    narrow_s,
    sends,
    receives,
):
    lon, lat = lax.axis_index("lon"), lax.axis_index("lat")
    core, far, far_count = lax.rem(lon, 2), lon // 2, lon_count // 2
    half = result.shape[0] // 2
    part = half // lat_count
    chunk = part // far_count

    def across(distance):
        return {"lon": lon, "lat": lax.rem(lat + distance + lat_count, lat_count)}

    def along(distance):
        other = lax.rem(far + distance + far_count, far_count)
        return {"lon": other * 2 + core, "lat": lat}

    twin = {"lon": far * 2 + 1 - core, "lat": lat}
    west, east = lax.rem(lon + lon_count - 1, lon_count), lax.rem(lon + 1, lon_count)
    north, south = lax.rem(lat + lat_count - 1, lat_count), lax.rem(lat + 1, lat_count)
    rim_to = [
        {"lon": west, "lat": lat},
        {"lon": lon, "lat": north},
        {"lon": west, "lat": north},
    ]
    rim_from = [
        {"lon": east, "lat": lat},
        {"lon": lon, "lat": south},
        {"lon": east, "lat": south},
    ]
    greeted = [twin] + [across(d) for d in range(1, lat_count)]
    greeted += [along(d) for d in range(1, far_count)] + rim_to + rim_from
    barrier = pltpu.get_barrier_semaphore()
    for device in greeted:
        pl.semaphore_signal(barrier, inc=1, device_id=device, device_id_type=pl.DeviceIdType.MESH)
    pl.semaphore_wait(barrier, len(greeted))

    used = []

    def send(source, target, device):
        slot = len(used)
        copy = pltpu.make_async_remote_copy(
            src_ref=source,
            dst_ref=target,
            send_sem=sends.at[slot],
            recv_sem=receives.at[slot],
            device_id=device,
            device_id_type=pl.DeviceIdType.MESH,
        )
        copy.start()
        used.append(copy)
        return copy

    def rows(index, size):
        return pl.ds(pl.multiple_of(index * size, 16), size)

    first = send(totals_ref.at[rows(1 - core, half)], core_in, twin)
    rims = []
    at = 0
    for length, device in zip(rim_parts, rim_to):
        window = pl.ds(at, length)
        rims.append(send(rim_ref.at[window], rim_in.at[window], device))
        at += length
    first.wait_recv()
    half_s[...] = (totals_ref[rows(core, half), :].astype(F32) + core_in[...].astype(F32)).astype(BF16)

    copies = []
    for d in range(1, lat_count):
        target = lax.rem(lat + d, lat_count)
        copies.append(send(half_s.at[rows(target, part)], lat_in.at[d - 1], across(d)))
    total = half_s[rows(lat, part), :].astype(F32)
    for d, copy in enumerate(copies):
        copy.wait_recv()
        total = total + lat_in[d].astype(F32)
    part_s[...] = total.astype(BF16)

    copies = []
    for d in range(1, far_count):
        target = lax.rem(far + d, far_count)
        copies.append(send(part_s.at[rows(target, chunk)], far_in.at[d - 1], along(d)))
    total = part_s[rows(far, chunk), :].astype(F32)
    for d, copy in enumerate(copies):
        copy.wait_recv()
        total = total + far_in[d].astype(F32)
    mine = rows((core * lat_count + lat) * far_count + far, chunk)
    result[mine, :] = total.astype(BF16)

    copies = [send(result.at[mine], result.at[mine], along(d)) for d in range(1, far_count)]
    for copy in copies:
        copy.wait_recv()
    mine = rows(core * lat_count + lat, part)
    copies = [send(result.at[mine], result.at[mine], across(d)) for d in range(1, lat_count)]
    for copy in copies:
        copy.wait_recv()
    mine = rows(core, half)
    last = send(result.at[mine], result.at[mine], twin)
    for copy in rims:
        copy.wait_recv()
    rim_out_ref[...] = rim_in[...]
    last.wait_recv()

    for t in range(4 * C // LANES):
        narrow_s[:, t * LANES : (t + 1) * LANES] = result[t * C : (t + 1) * C, :].astype(F32)
    grad_qkv_ref[...] = narrow_s[:, : 3 * C].astype(BF16)
    grad_proj_ref[...] = narrow_s[:, 3 * C :].astype(BF16)
    for t in range(FF // LANES):
        grad_up_ref[:, t * LANES : (t + 1) * LANES] = result[UP_AT + t * C : UP_AT + (t + 1) * C, :]
    grad_down_ref[:, :LANES] = result[DOWN_AT : DOWN_AT + FF, :]
    pair = result[PAIR_AT : PAIR_AT + FF // 2, :].astype(F32)
    grad_down_ref[: FF // 2, LANES:] = pair[:, : C - LANES].astype(BF16)
    grad_down_ref[FF // 2 :, LANES:] = pair[:, C - LANES :].astype(BF16)
    for copy in used:
        copy.wait_send()


def merge_patches(final, merge_weight):
    level_count, row_count, col_count, feat_count = final.shape
    grouped = final.reshape(level_count, row_count // 2, 2, col_count // 2, 2, feat_count)
    grouped = grouped.transpose(0, 1, 3, 2, 4, 5).reshape(-1, 4 * feat_count)
    center, inverse = center_of(grouped.astype(F32))
    merged = nn((center * inverse).astype(BF16), merge_weight).astype(BF16)
    return merged.reshape(level_count, row_count // 2, col_count // 2, 2 * feat_count)


def per_device(
    tokens,
    cotangent,
    qkv_codes,
    proj_codes,
    up_codes,
    down_codes,
    bit_widths,
    quant_scales,
    bias_table,
    bias_index,
    merge_weight,
):
    level_count, row_count, col_count, feat_count = tokens.shape
    token_count = level_count * row_count * col_count
    window_rows = row_count // WLAT
    grid_shape = (level_count, row_count, col_count)
    lat_limit = lax.axis_size("lat") * row_count - LAT_PAD
    lat_index = lax.axis_index("lat")
    lat_start = lat_index * row_count - WLAT // 2
    row_ids = lat_index * row_count + jnp.arange(row_count, dtype=jnp.int32)
    row_mask = (row_ids < lat_limit)[None, :, None, None]

    both = jnp.concatenate([tokens, cotangent], axis=-1)
    both = jnp.where(row_mask, both, jnp.zeros_like(both))
    frame = pull_rim(both).reshape(token_count, 2 * feat_count)

    pair = bias_index.reshape(2, HALF, 2, HALF)
    index = jnp.concatenate([pair[0, :, 0], pair[1, :, 1]], axis=0)
    index = jnp.pad(index, ((0, 0), (0, LANES - HALF)))
    positions = bias_table.shape[-1]
    pieces = -(-positions // LANES)
    table = bias_table.reshape(window_rows * HEADS, positions).astype(F32)
    table = jnp.pad(table, ((0, 0), (0, pieces * LANES - positions)))
    table = table.reshape(window_rows * HEADS, pieces, LANES)
    vmem = pl.BlockSpec(memory_space=pltpu.VMEM)
    smem = pl.BlockSpec(memory_space=pltpu.SMEM)
    bias = pl.pallas_call(
        functools.partial(gather_kernel, pieces),
        out_shape=jax.ShapeDtypeStruct((window_rows * HEADS, WTOK, LANES), F32),
        in_specs=[vmem, vmem],
        out_specs=vmem,
        compiler_params=pltpu.CompilerParams(vmem_limit_bytes=32 * 2**20),
        cost_estimate=pl.CostEstimate(flops=10**9, bytes_accessed=4 * 10**6, transcendentals=0),
        name="bias_gather",
    )(index, table)

    first_row = lat_start + WLAT * jnp.arange(window_rows, dtype=jnp.int32)
    edges = jnp.stack([-first_row * WLON, (lat_limit - first_row) * WLON], axis=1).reshape(-1)
    wide = jax.ShapeDtypeStruct((token_count, feat_count), BF16)
    lon_count, lat_count = lax.axis_size("lon"), lax.axis_size("lat")
    chunk = -(-TOTAL_ROWS // (lon_count * lat_count * 16)) * 16
    total_rows = chunk * lon_count * lat_count
    final, grad, totals = pl.pallas_call(
        functools.partial(block_kernel, window_rows),
        out_shape=[wide, wide, jax.ShapeDtypeStruct((total_rows, LANES), BF16)],
        in_specs=[smem] * 3 + [vmem] * 7,
        out_specs=[vmem] * 3,
        scratch_shapes=[pltpu.VMEM((token_count, feat_count), F32)] * 4
        + [pltpu.VMEM((C, 4 * C), F32), pltpu.VMEM((FF // 2, LANES), F32)],
        compiler_params=pltpu.CompilerParams(vmem_limit_bytes=48 * 2**20),
        name="block",
    )(
        edges,
        bit_widths,
        quant_scales,
        frame[:, :feat_count],
        frame[:, feat_count:],
        qkv_codes,
        proj_codes,
        up_codes,
        down_codes,
        bias,
    )
    frame = jnp.concatenate([final, grad], axis=-1).reshape(grid_shape + (-1,))
    rim_rows, rim_cols = WLAT // 2, WLON // 2
    cuts = [
        frame[:, rim_rows:, :rim_cols],
        frame[:, :rim_rows, rim_cols:],
        frame[:, :rim_rows, :rim_cols],
    ]
    flat = [cut.reshape(-1, 2 * feat_count) for cut in cuts]
    lengths = [-(-cut.shape[0] // 16) * 16 for cut in flat]
    rim = jnp.concatenate(
        [jnp.pad(cut, ((0, n - cut.shape[0]), (0, 0))) for cut, n in zip(flat, lengths)], axis=0
    )
    copies = 2 * (1 + lat_count - 1 + lon_count // 2 - 1) + len(cuts)
    half = total_rows // 2
    part = half // lat_count
    *grads, rim = pl.pallas_call(
        functools.partial(reduce_kernel, lon_count, lat_count, lengths),
        out_shape=[
            jax.ShapeDtypeStruct((C, 3 * C), BF16),
            jax.ShapeDtypeStruct((C, C), BF16),
            jax.ShapeDtypeStruct((C, FF), BF16),
            jax.ShapeDtypeStruct((FF, C), BF16),
            jax.ShapeDtypeStruct(rim.shape, BF16),
        ],
        in_specs=[vmem] * 2,
        out_specs=[vmem] * 5,
        scratch_shapes=[
            pltpu.VMEM((half, LANES), BF16),
            pltpu.VMEM((lat_count - 1, part, LANES), BF16),
            pltpu.VMEM((lon_count // 2 - 1, chunk, LANES), BF16),
            pltpu.VMEM((half, LANES), BF16),
            pltpu.VMEM((part, LANES), BF16),
            pltpu.VMEM((total_rows, LANES), BF16),
            pltpu.VMEM(rim.shape, BF16),
            pltpu.VMEM((C, 4 * C), F32),
            pltpu.SemaphoreType.DMA((copies,)),
            pltpu.SemaphoreType.DMA((copies,)),
        ],
        compiler_params=pltpu.CompilerParams(
            collective_id=0, has_side_effects=True, vmem_limit_bytes=48 * 2**20
        ),
        name="reduce_and_push",
    )(totals, rim)
    at = 0
    got = []
    for cut, source, n in zip(cuts, flat, lengths):
        got.append(rim[at : at + source.shape[0]].reshape(cut.shape))
        at += n
    upper = jnp.concatenate([frame[:, rim_rows:, rim_cols:], got[0]], axis=2)
    lower = jnp.concatenate([got[1], got[2]], axis=2)
    owned = jnp.concatenate([upper, lower], axis=1)
    owned = jnp.where(row_mask, owned, jnp.zeros_like(owned))
    merged = merge_patches(owned[..., :feat_count], merge_weight)
    return (merged, owned[..., feat_count:]) + tuple(grads)


def solution(mesh):
    split = P(None, "lat", "lon", None)
    placed = (split, split, P(), P(), P(), P(), P(), P(), P("lat", None, None, None), P(), P())
    return jax.shard_map(
        per_device,
        mesh=mesh,
        in_specs=placed,
        out_specs=(split, split, P(), P(), P(), P()),
        check_vma=False,
    )
```

```python
import functools
import math

import jax
import jax.numpy as jnp
from jax import lax
from jax.experimental import pallas as pl
from jax.experimental.pallas import tpu as pltpu
from jax.sharding import PartitionSpec as P

C = 192
HEADS = 6
FF = 768
HEAD_DIM = 32
WLAT = 6
WLON = 12
LAT_PAD = 11
WTOK = 144
HALF = 72
LANES = 128
PIECE = 256
STEPS = 12
EPSILON = 1e-05
MASKED = -1000000000.0
UP_AT = 6 * C
DOWN_AT = 12 * C
PAIR_AT = 16 * C
TOTAL_ROWS = 18 * C
F32 = jnp.float32
BF16 = jnp.bfloat16


def nn(left, right):
    return lax.dot_general(left, right, (((1,), (0,)), ((), ())), preferred_element_type=F32)


def nt(left, right):
    return lax.dot_general(left, right, (((1,), (1,)), ((), ())), preferred_element_type=F32)


def tn(left, right):
    return lax.dot_general(left, right, (((0,), (0,)), ((), ())), preferred_element_type=F32)


def neighbours(lon_count, lat_count):
    lon, lat = lax.axis_index("lon"), lax.axis_index("lat")
    west, east = lax.rem(lon + lon_count - 1, lon_count), lax.rem(lon + 1, lon_count)
    north, south = lax.rem(lat + lat_count - 1, lat_count), lax.rem(lat + 1, lat_count)
    behind = [{"lon": west, "lat": lat}, {"lon": lon, "lat": north}, {"lon": west, "lat": north}]
    ahead = [{"lon": east, "lat": lat}, {"lon": lon, "lat": south}, {"lon": east, "lat": south}]
    return behind, ahead


def greet(devices):
    barrier = pltpu.get_barrier_semaphore()
    for device in devices:
        pl.semaphore_signal(barrier, inc=1, device_id=device, device_id_type=pl.DeviceIdType.MESH)
    pl.semaphore_wait(barrier, len(devices))


def pull_kernel(
    lon_count,
    lat_count,
    rim_parts,
    rim_ref,
    index_ref,
    table_ref,
    rim_out_ref,
    bias_ref,
    rim_in,
    sends,
    receives,
):
    behind, ahead = neighbours(lon_count, lat_count)
    greet(behind + ahead)
    copies = []
    at = 0
    for slot, (length, device) in enumerate(zip(rim_parts, ahead)):
        copy = pltpu.make_async_remote_copy(
            src_ref=rim_ref.at[pl.ds(at, length)],
            dst_ref=rim_in.at[pl.ds(at, length)],
            send_sem=sends.at[slot],
            recv_sem=receives.at[slot],
            device_id=device,
            device_id_type=pl.DeviceIdType.MESH,
        )
        copy.start()
        copies.append(copy)
        at += length

    steps, width = index_ref.shape
    table_rows = bias_ref.shape[0]
    pieces, piece_rows, piece = table_ref.shape
    tables = table_ref[...].reshape(pieces * piece_rows, piece)
    inside = lax.broadcasted_iota(jnp.int32, (piece, width), 0)

    def one_step(step, carry):
        index = index_ref[pl.ds(step, 1), :]
        low = jnp.bitwise_and(index, piece - 1)
        high = jnp.right_shift(index, piece.bit_length() - 1)
        chosen = jnp.where(inside == low, 1.0, 0.0).astype(BF16)
        found = nn(tables, chosen)
        total = found[:piece_rows]
        for p in range(1, pieces):
            total = jnp.where(high == p, found[p * piece_rows : (p + 1) * piece_rows], total)
        for i in range(width // LANES):
            for r in range(table_rows):
                row = total[r : r + 1, i * LANES : (i + 1) * LANES]
                bias_ref[r, pl.ds(step * (width // LANES) + i, 1), :] = row
        return carry

    lax.fori_loop(0, steps, one_step, 0)
    for copy in copies:
        copy.wait_recv()
    rim_out_ref[...] = rim_in[...]
    for copy in copies:
        copy.wait_send()


def center_of(values):
    center = values - jnp.mean(values, axis=-1, keepdims=True)
    spread = jnp.mean(center * center, axis=-1, keepdims=True)
    return center, lax.rsqrt(spread + EPSILON)


def norm_back(center, scale, upstream):
    inner = jnp.mean(upstream * center, axis=-1, keepdims=True)
    outer = jnp.mean(upstream, axis=-1, keepdims=True)
    return scale * (upstream - outer - center * (scale * scale * inner))


def block_kernel(
    window_rows,
    edges_ref,
    bits_ref,
    scales_ref,
    start_ref,
    d_out_ref,
    qkv_ref,
    proj_ref,
    up_ref,
    down_ref,
    bias_ref,
    final_ref,
    grad_ref,
    totals_ref,
    heads_s,
    dq_s,
    dk_s,
    dv_s,
    narrow_s,
    pair_s,
):
    def dequant(codes, layer, fan_in):
        largest = jnp.left_shift(jnp.int32(1), bits_ref[layer] - 1) - 1
        scale = jnp.full((1, codes.shape[1]), scales_ref[layer].astype(F32), F32)
        factor = math.sqrt(C / fan_in) / scale
        return (jnp.clip(codes, -largest, largest).astype(F32) * factor).astype(BF16)

    w_q = dequant(qkv_ref[:, :C], 0, C)
    w_k = dequant(qkv_ref[:, C : 2 * C], 0, C)
    w_v = dequant(qkv_ref[:, 2 * C :], 0, C)
    w_proj = dequant(proj_ref[...], 1, C)
    start = start_ref[...].astype(F32)
    center, inverse = center_of(start)
    normed = (center * inverse).astype(BF16)
    q = nn(normed, w_q).astype(BF16)
    k = nn(normed, w_k).astype(BF16)
    v = nn(normed, w_v).astype(BF16)

    lane = lax.broadcasted_iota(jnp.int32, (HALF, C), 1)
    head_masks = [(lane >= h * HEAD_DIM) & (lane < (h + 1) * HEAD_DIM) for h in range(HEADS)]

    def stack(values):
        wide = values.astype(F32)
        return jnp.concatenate([jnp.where(m, wide, 0.0) for m in head_masks], axis=0).astype(BF16)

    def unstack(values):
        total = jnp.zeros((HALF, C), F32)
        for h, m in enumerate(head_masks):
            total = jnp.where(m, values[h * HALF : (h + 1) * HALF], total)
        return total

    keys = lax.broadcasted_iota(jnp.int32, (HEADS * HALF, HALF), 1)
    blocks = start.shape[0] // HALF
    saved = []
    for b in range(blocks):
        level, a = b // window_rows, b % window_rows
        part = slice(b * HALF, (b + 1) * HALF)
        stacked_q = stack(q[part])
        bias = bias_ref[a * HEADS : (a + 1) * HEADS, (1 - level) * HALF : (2 - level) * HALF, :]
        bias = bias.reshape(HEADS * HALF, LANES)[:, :HALF]
        scores = nt(stacked_q, k[part]) * HEAD_DIM ** (-0.5) + bias
        allowed = (keys >= edges_ref[2 * a]) & (keys < edges_ref[2 * a + 1])
        scores = jnp.where(allowed, scores, MASKED)
        weights = jnp.exp(scores - jnp.max(scores, axis=-1, keepdims=True))
        weights = weights / jnp.sum(weights, axis=-1, keepdims=True)
        saved.append((stacked_q, weights, allowed))
        heads_s[part, :] = unstack(nn(weights.astype(BF16), v[part]))

    heads = heads_s[...].astype(BF16)
    resid = (start + nn(heads, w_proj)).astype(BF16)
    center_two, inverse_two = center_of(resid.astype(F32))
    normed_two = (center_two * inverse_two).astype(BF16)
    w_up = dequant(up_ref[...], 2, C)
    w_down = dequant(down_ref[...], 3, FF)
    pre = nn(normed_two, w_up)
    cubic = math.sqrt(2 / math.pi)
    square = pre * pre
    bent = jnp.tanh(cubic * (pre + 0.044715 * square * pre))
    hidden = (0.5 * pre * (1.0 + bent)).astype(BF16)
    final_ref[...] = (resid.astype(F32) + nn(hidden, w_down)).astype(BF16)
    d_out = d_out_ref[...]
    down_total = tn(hidden, d_out)
    totals_ref[DOWN_AT : DOWN_AT + FF, :] = down_total[:, :LANES].astype(BF16)
    pair_s[:, : C - LANES] = down_total[: FF // 2, LANES:]
    pair_s[:, C - LANES :] = down_total[FF // 2 :, LANES:]
    totals_ref[PAIR_AT : PAIR_AT + FF // 2, :] = pair_s[...].astype(BF16)
    d_hidden = nt(d_out, w_down).astype(BF16).astype(F32)
    slope = 0.5 * (1.0 + bent) + 0.5 * pre * (1.0 - bent * bent) * cubic * (
        1.0 + 3 * 0.044715 * square
    )
    d_pre = (slope * d_hidden).astype(BF16)
    up_total = tn(normed_two, d_pre).astype(BF16)
    for t in range(FF // LANES):
        totals_ref[UP_AT + t * C : UP_AT + (t + 1) * C, :] = up_total[:, t * LANES : (t + 1) * LANES]
    d_normed_two = nt(d_pre, w_up).astype(BF16).astype(F32)
    d_resid = (d_out.astype(F32) + norm_back(center_two, inverse_two, d_normed_two)).astype(BF16)
    narrow_s[:, 3 * C :] = tn(heads, d_resid)
    d_heads = nt(d_resid, w_proj).astype(BF16)

    for b in range(blocks):
        part = slice(b * HALF, (b + 1) * HALF)
        stacked_q, weights, allowed = saved[b]
        d_stacked = stack(d_heads[part])
        d_weights = nt(d_stacked, v[part]).astype(BF16).astype(F32)
        dv_s[part, :] = tn(weights.astype(BF16), d_stacked)
        inner = jnp.sum(weights * d_weights, axis=-1, keepdims=True)
        d_scores = jnp.where(allowed, weights * (d_weights - inner), 0.0)
        d_scores = (d_scores * HEAD_DIM ** (-0.5)).astype(BF16)
        dq_s[part, :] = unstack(nn(d_scores, k[part]))
        dk_s[part, :] = tn(d_scores, stacked_q)

    dq = dq_s[...].astype(BF16)
    dk = dk_s[...].astype(BF16)
    dv = dv_s[...].astype(BF16)
    narrow_s[:, :C] = tn(normed, dq)
    narrow_s[:, C : 2 * C] = tn(normed, dk)
    narrow_s[:, 2 * C : 3 * C] = tn(normed, dv)
    for t in range(4 * C // LANES):
        tile = narrow_s[:, t * LANES : (t + 1) * LANES]
        totals_ref[t * C : (t + 1) * C, :] = tile.astype(BF16)
    spare = totals_ref.shape[0] - TOTAL_ROWS
    if spare:
        totals_ref[TOTAL_ROWS:, :] = jnp.zeros((spare, LANES), BF16)
    d_normed = (nt(dq, w_q) + nt(dk, w_k) + nt(dv, w_v)).astype(BF16).astype(F32)
    grad_ref[...] = (d_resid.astype(F32) + norm_back(center, inverse, d_normed)).astype(BF16)


def reduce_kernel(
    lon_count,
    lat_count,
    rim_parts,
    totals_ref,
    rim_ref,
    grad_qkv_ref,
    grad_proj_ref,
    grad_up_ref,
    grad_down_ref,
    rim_out_ref,
    core_in,
    lat_in,
    far_in,
    half_s,
    part_s,
    result,
    rim_in,
    narrow_s,
    sends,
    receives,
):
    lon, lat = lax.axis_index("lon"), lax.axis_index("lat")
    core, far, far_count = lax.rem(lon, 2), lon // 2, lon_count // 2
    half = result.shape[0] // 2
    part = half // lat_count
    chunk = part // far_count

    def across(distance):
        return {"lon": lon, "lat": lax.rem(lat + distance + lat_count, lat_count)}

    def along(distance):
        other = lax.rem(far + distance + far_count, far_count)
        return {"lon": other * 2 + core, "lat": lat}

    twin = {"lon": far * 2 + 1 - core, "lat": lat}
    rim_to, rim_from = neighbours(lon_count, lat_count)
    greeted = [twin] + [across(d) for d in range(1, lat_count)]
    greeted += [along(d) for d in range(1, far_count)] + rim_to + rim_from
    greet(greeted)

    used = []

    def send(source, target, device):
        slot = len(used)
        copy = pltpu.make_async_remote_copy(
            src_ref=source,
            dst_ref=target,
            send_sem=sends.at[slot],
            recv_sem=receives.at[slot],
            device_id=device,
            device_id_type=pl.DeviceIdType.MESH,
        )
        copy.start()
        used.append(copy)
        return copy

    def rows(index, size):
        return pl.ds(pl.multiple_of(index * size, 16), size)

    first = send(totals_ref.at[rows(1 - core, half)], core_in, twin)
    rims = []
    at = 0
    for length, device in zip(rim_parts, rim_to):
        window = pl.ds(at, length)
        rims.append(send(rim_ref.at[window], rim_in.at[window], device))
        at += length
    first.wait_recv()
    half_s[...] = (totals_ref[rows(core, half), :].astype(F32) + core_in[...].astype(F32)).astype(BF16)

    copies = []
    for d in range(1, lat_count):
        target = lax.rem(lat + d, lat_count)
        copies.append(send(half_s.at[rows(target, part)], lat_in.at[d - 1], across(d)))
    total = half_s[rows(lat, part), :].astype(F32)
    for d, copy in enumerate(copies):
        copy.wait_recv()
        total = total + lat_in[d].astype(F32)
    part_s[...] = total.astype(BF16)

    copies = []
    for d in range(1, far_count):
        target = lax.rem(far + d, far_count)
        copies.append(send(part_s.at[rows(target, chunk)], far_in.at[d - 1], along(d)))
    total = part_s[rows(far, chunk), :].astype(F32)
    for d, copy in enumerate(copies):
        copy.wait_recv()
        total = total + far_in[d].astype(F32)
    mine = rows((core * lat_count + lat) * far_count + far, chunk)
    result[mine, :] = total.astype(BF16)

    copies = [send(result.at[mine], result.at[mine], along(d)) for d in range(1, far_count)]
    for copy in copies:
        copy.wait_recv()
    mine = rows(core * lat_count + lat, part)
    copies = [send(result.at[mine], result.at[mine], across(d)) for d in range(1, lat_count)]
    for copy in copies:
        copy.wait_recv()
    mine = rows(core, half)
    last = send(result.at[mine], result.at[mine], twin)
    for copy in rims:
        copy.wait_recv()
    rim_out_ref[...] = rim_in[...]
    last.wait_recv()

    for t in range(4 * C // LANES):
        narrow_s[:, t * LANES : (t + 1) * LANES] = result[t * C : (t + 1) * C, :].astype(F32)
    grad_qkv_ref[...] = narrow_s[:, : 3 * C].astype(BF16)
    grad_proj_ref[...] = narrow_s[:, 3 * C :].astype(BF16)
    for t in range(FF // LANES):
        grad_up_ref[:, t * LANES : (t + 1) * LANES] = result[UP_AT + t * C : UP_AT + (t + 1) * C, :]
    grad_down_ref[:, :LANES] = result[DOWN_AT : DOWN_AT + FF, :]
    pair = result[PAIR_AT : PAIR_AT + FF // 2, :].astype(F32)
    grad_down_ref[: FF // 2, LANES:] = pair[:, : C - LANES].astype(BF16)
    grad_down_ref[FF // 2 :, LANES:] = pair[:, C - LANES :].astype(BF16)
    for copy in used:
        copy.wait_send()


def merge_patches(final, merge_weight):
    level_count, row_count, col_count, feat_count = final.shape
    grouped = final.reshape(level_count, row_count // 2, 2, col_count // 2, 2, feat_count)
    grouped = grouped.transpose(0, 1, 3, 2, 4, 5).reshape(-1, 4 * feat_count)
    center, inverse = center_of(grouped.astype(F32))
    merged = nn((center * inverse).astype(BF16), merge_weight).astype(BF16)
    return merged.reshape(level_count, row_count // 2, col_count // 2, 2 * feat_count)


def packed(cuts):
    flat = [cut.reshape(-1, cut.shape[-1]) for cut in cuts]
    lengths = [-(-cut.shape[0] // 16) * 16 for cut in flat]
    padded = [jnp.pad(cut, ((0, n - cut.shape[0]), (0, 0))) for cut, n in zip(flat, lengths)]

    def unpack(buffer):
        starts = [sum(lengths[:i]) for i in range(len(cuts))]
        return [
            buffer[at : at + part.shape[0]].reshape(cut.shape)
            for at, part, cut in zip(starts, flat, cuts)
        ]

    return jnp.concatenate(padded, axis=0), lengths, unpack


def per_device(
    tokens,
    cotangent,
    qkv_codes,
    proj_codes,
    up_codes,
    down_codes,
    bit_widths,
    quant_scales,
    bias_table,
    bias_index,
    merge_weight,
):
    level_count, row_count, col_count, feat_count = tokens.shape
    token_count = level_count * row_count * col_count
    window_rows = row_count // WLAT
    grid_shape = (level_count, row_count, col_count)
    lat_limit = lax.axis_size("lat") * row_count - LAT_PAD
    lat_index = lax.axis_index("lat")
    lat_start = lat_index * row_count - WLAT // 2
    row_ids = lat_index * row_count + jnp.arange(row_count, dtype=jnp.int32)
    row_mask = (row_ids < lat_limit)[None, :, None, None]

    both = jnp.concatenate([tokens, cotangent], axis=-1)
    both = jnp.where(row_mask, both, jnp.zeros_like(both))
    lon_count, lat_count = lax.axis_size("lon"), lax.axis_size("lat")
    rim_rows, rim_cols = WLAT // 2, WLON // 2
    pulled, lengths, unpack = packed(
        [both[:, :-rim_rows, rim_cols:], both[:, -rim_rows:, :rim_cols], both[:, -rim_rows:, rim_cols:]]
    )
    pair = bias_index.reshape(2, HALF, 2, HALF)
    index = jnp.concatenate([pair[0, :, 0], pair[1, :, 1]], axis=0)
    index = jnp.pad(index, ((0, 0), (0, LANES - HALF))).reshape(STEPS, -1)
    positions = bias_table.shape[-1]
    table_rows = window_rows * HEADS
    pieces, piece_rows = -(-positions // PIECE), -(-table_rows // 16) * 16
    table = bias_table.reshape(table_rows, positions)
    spare = ((0, piece_rows - table_rows), (0, pieces * PIECE - positions))
    table = jnp.pad(table, spare).reshape(piece_rows, pieces, PIECE).transpose(1, 0, 2)
    vmem = pl.BlockSpec(memory_space=pltpu.VMEM)
    smem = pl.BlockSpec(memory_space=pltpu.SMEM)
    pulled, bias = pl.pallas_call(
        functools.partial(pull_kernel, lon_count, lat_count, lengths),
        out_shape=[
            jax.ShapeDtypeStruct(pulled.shape, BF16),
            jax.ShapeDtypeStruct((table_rows, WTOK, LANES), F32),
        ],
        in_specs=[vmem] * 3,
        out_specs=[vmem] * 2,
        scratch_shapes=[
            pltpu.VMEM(pulled.shape, BF16),
            pltpu.SemaphoreType.DMA((len(lengths),)),
            pltpu.SemaphoreType.DMA((len(lengths),)),
        ],
        compiler_params=pltpu.CompilerParams(
            collective_id=1, has_side_effects=True, vmem_limit_bytes=32 * 2**20
        ),
        name="pull_and_bias",
    )(pulled, index, table)
    got = unpack(pulled)
    upper = jnp.concatenate([got[2], got[1]], axis=2)
    lower = jnp.concatenate([got[0], both[:, :-rim_rows, :rim_cols]], axis=2)
    frame = jnp.concatenate([upper, lower], axis=1).reshape(token_count, 2 * feat_count)

    first_row = lat_start + WLAT * jnp.arange(window_rows, dtype=jnp.int32)
    edges = jnp.stack([-first_row * WLON, (lat_limit - first_row) * WLON], axis=1).reshape(-1)
    wide = jax.ShapeDtypeStruct((token_count, feat_count), BF16)
    chunk = -(-TOTAL_ROWS // (lon_count * lat_count * 16)) * 16
    total_rows = chunk * lon_count * lat_count
    final, grad, totals = pl.pallas_call(
        functools.partial(block_kernel, window_rows),
        out_shape=[wide, wide, jax.ShapeDtypeStruct((total_rows, LANES), BF16)],
        in_specs=[smem] * 3 + [vmem] * 7,
        out_specs=[vmem] * 3,
        scratch_shapes=[pltpu.VMEM((token_count, feat_count), F32)] * 4
        + [pltpu.VMEM((C, 4 * C), F32), pltpu.VMEM((FF // 2, LANES), F32)],
        compiler_params=pltpu.CompilerParams(vmem_limit_bytes=48 * 2**20),
        name="block",
    )(
        edges,
        bit_widths,
        quant_scales,
        frame[:, :feat_count],
        frame[:, feat_count:],
        qkv_codes,
        proj_codes,
        up_codes,
        down_codes,
        bias,
    )
    frame = jnp.concatenate([final, grad], axis=-1).reshape(grid_shape + (-1,))
    rim, lengths, unpack = packed(
        [frame[:, rim_rows:, :rim_cols], frame[:, :rim_rows, rim_cols:], frame[:, :rim_rows, :rim_cols]]
    )
    copies = 2 * (1 + lat_count - 1 + lon_count // 2 - 1) + len(lengths)
    half = total_rows // 2
    part = half // lat_count
    *grads, rim = pl.pallas_call(
        functools.partial(reduce_kernel, lon_count, lat_count, lengths),
        out_shape=[
            jax.ShapeDtypeStruct((C, 3 * C), BF16),
            jax.ShapeDtypeStruct((C, C), BF16),
            jax.ShapeDtypeStruct((C, FF), BF16),
            jax.ShapeDtypeStruct((FF, C), BF16),
            jax.ShapeDtypeStruct(rim.shape, BF16),
        ],
        in_specs=[vmem] * 2,
        out_specs=[vmem] * 5,
        scratch_shapes=[
            pltpu.VMEM((half, LANES), BF16),
            pltpu.VMEM((lat_count - 1, part, LANES), BF16),
            pltpu.VMEM((lon_count // 2 - 1, chunk, LANES), BF16),
            pltpu.VMEM((half, LANES), BF16),
            pltpu.VMEM((part, LANES), BF16),
            pltpu.VMEM((total_rows, LANES), BF16),
            pltpu.VMEM(rim.shape, BF16),
            pltpu.VMEM((C, 4 * C), F32),
            pltpu.SemaphoreType.DMA((copies,)),
            pltpu.SemaphoreType.DMA((copies,)),
        ],
        compiler_params=pltpu.CompilerParams(
            collective_id=0, has_side_effects=True, vmem_limit_bytes=48 * 2**20
        ),
        name="reduce_and_push",
    )(totals, rim)
    got = unpack(rim)
    upper = jnp.concatenate([frame[:, rim_rows:, rim_cols:], got[0]], axis=2)
    lower = jnp.concatenate([got[1], got[2]], axis=2)
    owned = jnp.concatenate([upper, lower], axis=1)
    owned = jnp.where(row_mask, owned, jnp.zeros_like(owned))
    merged = merge_patches(owned[..., :feat_count], merge_weight)
    return (merged, owned[..., feat_count:]) + tuple(grads)


def solution(mesh):
    split = P(None, "lat", "lon", None)
    placed = (split, split, P(), P(), P(), P(), P(), P(), P("lat", None, None, None), P(), P())
    return jax.shard_map(
        per_device,
        mesh=mesh,
        in_specs=placed,
        out_specs=(split, split, P(), P(), P(), P()),
        check_vma=False,
    )
```

```python
import functools
import math

import jax
import jax.numpy as jnp
from jax import lax
from jax.experimental import pallas as pl
from jax.experimental.pallas import tpu as pltpu
from jax.sharding import PartitionSpec as P

C = 192
HEADS = 6
FF = 768
HEAD_DIM = 32
WLAT = 6
WLON = 12
LAT_PAD = 11
WTOK = 144
HALF = 72
LANES = 128
PIECE = 256
STEPS = 12
EPSILON = 1e-05
MASKED = -1000000000.0
UP_AT = 6 * C
DOWN_AT = 12 * C
TOTAL_ROWS = 18 * C
F32 = jnp.float32
BF16 = jnp.bfloat16


def nn(left, right):
    return lax.dot_general(left, right, (((1,), (0,)), ((), ())), preferred_element_type=F32)


def nt(left, right):
    return lax.dot_general(left, right, (((1,), (1,)), ((), ())), preferred_element_type=F32)


def tn(left, right):
    return lax.dot_general(left, right, (((0,), (0,)), ((), ())), preferred_element_type=F32)


def neighbours(lon_count, lat_count):
    lon, lat = lax.axis_index("lon"), lax.axis_index("lat")
    west, east = lax.rem(lon + lon_count - 1, lon_count), lax.rem(lon + 1, lon_count)
    north, south = lax.rem(lat + lat_count - 1, lat_count), lax.rem(lat + 1, lat_count)
    behind = [{"lon": west, "lat": lat}, {"lon": lon, "lat": north}, {"lon": west, "lat": north}]
    ahead = [{"lon": east, "lat": lat}, {"lon": lon, "lat": south}, {"lon": east, "lat": south}]
    return behind, ahead


def greet(devices):
    barrier = pltpu.get_barrier_semaphore()
    for device in devices:
        pl.semaphore_signal(barrier, inc=1, device_id=device, device_id_type=pl.DeviceIdType.MESH)
    pl.semaphore_wait(barrier, len(devices))


def pull_kernel(
    lon_count,
    lat_count,
    rim_parts,
    rim_ref,
    index_ref,
    table_ref,
    qkv_far,
    proj_far,
    up_far,
    down_far,
    rim_out_ref,
    bias_ref,
    qkv_ref,
    proj_ref,
    up_ref,
    down_ref,
    rim_in,
    sends,
    receives,
    fetches,
):
    pairs = [(qkv_far, qkv_ref), (proj_far, proj_ref), (up_far, up_ref), (down_far, down_ref)]
    fetched = []
    for slot, (source, target) in enumerate(pairs):
        fetched.append(pltpu.make_async_copy(source, target, fetches.at[slot]))
        fetched[-1].start()
    behind, ahead = neighbours(lon_count, lat_count)
    greet(behind + ahead)
    copies = []
    at = 0
    for slot, (length, device) in enumerate(zip(rim_parts, ahead)):
        copy = pltpu.make_async_remote_copy(
            src_ref=rim_ref.at[pl.ds(at, length)],
            dst_ref=rim_in.at[pl.ds(at, length)],
            send_sem=sends.at[slot],
            recv_sem=receives.at[slot],
            device_id=device,
            device_id_type=pl.DeviceIdType.MESH,
        )
        copy.start()
        copies.append(copy)
        at += length

    steps, width = index_ref.shape
    table_rows = bias_ref.shape[0]
    pieces, piece_rows, piece = table_ref.shape
    tables = table_ref[...].reshape(pieces * piece_rows, piece)
    inside = lax.broadcasted_iota(jnp.int32, (piece, width), 0)

    def one_step(step, carry):
        index = index_ref[pl.ds(step, 1), :]
        low = jnp.bitwise_and(index, piece - 1)
        high = jnp.right_shift(index, piece.bit_length() - 1)
        chosen = jnp.where(inside == low, 1.0, 0.0).astype(BF16)
        found = nn(tables, chosen)
        total = found[:piece_rows]
        for p in range(1, pieces):
            total = jnp.where(high == p, found[p * piece_rows : (p + 1) * piece_rows], total)
        for i in range(width // LANES):
            for r in range(table_rows):
                row = total[r : r + 1, i * LANES : (i + 1) * LANES]
                bias_ref[r, pl.ds(step * (width // LANES) + i, 1), :] = row
        return carry

    lax.fori_loop(0, steps, one_step, 0)
    for copy in fetched:
        copy.wait()
    for copy in copies:
        copy.wait_recv()
    rim_out_ref[...] = rim_in[...]
    for copy in copies:
        copy.wait_send()


def center_of(values):
    center = values - jnp.mean(values, axis=-1, keepdims=True)
    spread = jnp.mean(center * center, axis=-1, keepdims=True)
    return center, lax.rsqrt(spread + EPSILON)


def norm_back(center, scale, upstream):
    inner = jnp.mean(upstream * center, axis=-1, keepdims=True)
    outer = jnp.mean(upstream, axis=-1, keepdims=True)
    return scale * (upstream - outer - center * (scale * scale * inner))


def block_kernel(
    window_rows,
    scalars_ref,
    start_ref,
    d_out_ref,
    qkv_ref,
    proj_ref,
    up_ref,
    down_ref,
    bias_ref,
    final_ref,
    grad_ref,
    totals_ref,
    heads_s,
    dq_s,
    dk_s,
    dv_s,
    narrow_s,
):
    def dequant(codes, layer, fan_in):
        largest = jnp.left_shift(jnp.int32(1), scalars_ref[layer] - 1) - 1
        scale = jnp.full((1, codes.shape[1]), scalars_ref[4 + layer].astype(F32), F32)
        factor = math.sqrt(C / fan_in) / scale
        return (jnp.clip(codes, -largest, largest).astype(F32) * factor).astype(BF16)

    w_q = dequant(qkv_ref[:, :C], 0, C)
    w_k = dequant(qkv_ref[:, C : 2 * C], 0, C)
    w_v = dequant(qkv_ref[:, 2 * C :], 0, C)
    w_proj = dequant(proj_ref[...], 1, C)
    start = start_ref[...].astype(F32)
    center, inverse = center_of(start)
    normed = (center * inverse).astype(BF16)
    q = nn(normed, w_q).astype(BF16)
    k = nn(normed, w_k).astype(BF16)
    v = nn(normed, w_v).astype(BF16)

    lane = lax.broadcasted_iota(jnp.int32, (HALF, C), 1)
    head_masks = [(lane >= h * HEAD_DIM) & (lane < (h + 1) * HEAD_DIM) for h in range(HEADS)]

    def stack(values):
        wide = values.astype(F32)
        return jnp.concatenate([jnp.where(m, wide, 0.0) for m in head_masks], axis=0).astype(BF16)

    def unstack(values):
        total = jnp.zeros((HALF, C), F32)
        for h, m in enumerate(head_masks):
            total = jnp.where(m, values[h * HALF : (h + 1) * HALF], total)
        return total

    keys = lax.broadcasted_iota(jnp.int32, (HEADS * HALF, HALF), 1)
    blocks = start.shape[0] // HALF
    saved = []
    for b in range(blocks):
        level, a = b // window_rows, b % window_rows
        part = slice(b * HALF, (b + 1) * HALF)
        stacked_q = stack(q[part])
        bias = bias_ref[a * HEADS : (a + 1) * HEADS, (1 - level) * HALF : (2 - level) * HALF, :]
        bias = bias.reshape(HEADS * HALF, LANES)[:, :HALF]
        scores = nt(stacked_q, k[part]) * HEAD_DIM ** (-0.5) + bias
        allowed = (keys >= scalars_ref[8 + 2 * a]) & (keys < scalars_ref[9 + 2 * a])
        scores = jnp.where(allowed, scores, MASKED)
        weights = jnp.exp(scores - jnp.max(scores, axis=-1, keepdims=True))
        weights = weights / jnp.sum(weights, axis=-1, keepdims=True)
        saved.append((stacked_q, weights, allowed))
        heads_s[part, :] = unstack(nn(weights.astype(BF16), v[part]))

    heads = heads_s[...].astype(BF16)
    resid = (start + nn(heads, w_proj)).astype(BF16)
    center_two, inverse_two = center_of(resid.astype(F32))
    normed_two = (center_two * inverse_two).astype(BF16)
    w_up = dequant(up_ref[...], 2, C)
    w_down_t = dequant(down_ref[...], 3, FF)
    pre = nn(normed_two, w_up)
    cubic = math.sqrt(2 / math.pi)
    square = pre * pre
    bent = jnp.tanh(cubic * (pre + 0.044715 * square * pre))
    hidden = (0.5 * pre * (1.0 + bent)).astype(BF16)
    final_ref[...] = (resid.astype(F32) + nt(hidden, w_down_t)).astype(BF16)
    d_out = d_out_ref[...]
    down_total = tn(d_out, hidden).astype(BF16)
    for t in range(FF // LANES):
        rows = slice(DOWN_AT + t * C, DOWN_AT + (t + 1) * C)
        totals_ref[rows, :] = down_total[:, t * LANES : (t + 1) * LANES]
    d_hidden = nn(d_out, w_down_t).astype(BF16).astype(F32)
    slope = 0.5 * (1.0 + bent) + 0.5 * pre * (1.0 - bent * bent) * cubic * (
        1.0 + 3 * 0.044715 * square
    )
    d_pre = (slope * d_hidden).astype(BF16)
    up_total = tn(normed_two, d_pre).astype(BF16)
    for t in range(FF // LANES):
        totals_ref[UP_AT + t * C : UP_AT + (t + 1) * C, :] = up_total[:, t * LANES : (t + 1) * LANES]
    d_normed_two = nt(d_pre, w_up).astype(BF16).astype(F32)
    d_resid = (d_out.astype(F32) + norm_back(center_two, inverse_two, d_normed_two)).astype(BF16)
    narrow_s[:, 3 * C :] = tn(heads, d_resid)
    d_heads = nt(d_resid, w_proj).astype(BF16)

    for b in range(blocks):
        part = slice(b * HALF, (b + 1) * HALF)
        stacked_q, weights, allowed = saved[b]
        d_stacked = stack(d_heads[part])
        d_weights = nt(d_stacked, v[part]).astype(BF16).astype(F32)
        dv_s[part, :] = tn(weights.astype(BF16), d_stacked)
        inner = jnp.sum(weights * d_weights, axis=-1, keepdims=True)
        d_scores = jnp.where(allowed, weights * (d_weights - inner), 0.0)
        d_scores = (d_scores * HEAD_DIM ** (-0.5)).astype(BF16)
        dq_s[part, :] = unstack(nn(d_scores, k[part]))
        dk_s[part, :] = tn(d_scores, stacked_q)

    dq = dq_s[...].astype(BF16)
    dk = dk_s[...].astype(BF16)
    dv = dv_s[...].astype(BF16)
    narrow_s[:, :C] = tn(normed, dq)
    narrow_s[:, C : 2 * C] = tn(normed, dk)
    narrow_s[:, 2 * C : 3 * C] = tn(normed, dv)
    for t in range(4 * C // LANES):
        tile = narrow_s[:, t * LANES : (t + 1) * LANES]
        totals_ref[t * C : (t + 1) * C, :] = tile.astype(BF16)
    spare = totals_ref.shape[0] - TOTAL_ROWS
    if spare:
        totals_ref[TOTAL_ROWS:, :] = jnp.zeros((spare, LANES), BF16)
    d_normed = (nt(dq, w_q) + nt(dk, w_k) + nt(dv, w_v)).astype(BF16).astype(F32)
    grad_ref[...] = (d_resid.astype(F32) + norm_back(center, inverse, d_normed)).astype(BF16)


def reduce_kernel(
    lon_count,
    lat_count,
    rim_parts,
    chunks,
    totals_ref,
    rim_ref,
    grad_qkv_ref,
    grad_proj_ref,
    grad_up_ref,
    grad_down_ref,
    rim_out_ref,
    core_in,
    lat_in,
    far_in,
    half_s,
    part_s,
    result,
    rim_in,
    narrow_s,
    sends,
    receives,
):
    lon, lat = lax.axis_index("lon"), lax.axis_index("lat")
    core, far, far_count = lax.rem(lon, 2), lon // 2, lon_count // 2
    def across(distance):
        return {"lon": lon, "lat": lax.rem(lat + distance + lat_count, lat_count)}

    def along(distance):
        other = lax.rem(far + distance + far_count, far_count)
        return {"lon": other * 2 + core, "lat": lat}

    twin = {"lon": far * 2 + 1 - core, "lat": lat}
    rim_to, rim_from = neighbours(lon_count, lat_count)
    greeted = [twin] + [across(d) for d in range(1, lat_count)]
    greeted += [along(d) for d in range(1, far_count)] + rim_to + rim_from
    greet(greeted)

    used = []

    def send(source, target, device):
        slot = len(used)
        copy = pltpu.make_async_remote_copy(
            src_ref=source,
            dst_ref=target,
            send_sem=sends.at[slot],
            recv_sem=receives.at[slot],
            device_id=device,
            device_id_type=pl.DeviceIdType.MESH,
        )
        copy.start()
        used.append(copy)
        return copy

    def sum_piece(before, chunk):
        part = chunk * far_count
        half = part * lat_count
        part_at, half_at, whole_at = before * far_count, before * far_count * lat_count, 0
        whole_at = 2 * half_at

        def rows(start, index, size):
            return pl.ds(pl.multiple_of(start + index * size, 16), size)

        arriving = core_in.at[pl.ds(half_at, half)]
        first = send(totals_ref.at[rows(whole_at, 1 - core, half)], arriving, twin)
        yield
        first.wait_recv()
        total = totals_ref[rows(whole_at, core, half), :].astype(F32)
        total = total + core_in[pl.ds(half_at, half), :].astype(F32)
        half_s[pl.ds(half_at, half), :] = total.astype(BF16)
        copies = []
        for d in range(1, lat_count):
            source = half_s.at[rows(half_at, lax.rem(lat + d, lat_count), part)]
            copies.append(send(source, lat_in.at[d - 1, pl.ds(part_at, part)], across(d)))
        yield
        total = half_s[rows(half_at, lat, part), :].astype(F32)
        for d, copy in enumerate(copies):
            copy.wait_recv()
            total = total + lat_in[d, pl.ds(part_at, part), :].astype(F32)
        part_s[pl.ds(part_at, part), :] = total.astype(BF16)
        copies = []
        for d in range(1, far_count):
            source = part_s.at[rows(part_at, lax.rem(far + d, far_count), chunk)]
            copies.append(send(source, far_in.at[d - 1, pl.ds(before, chunk)], along(d)))
        yield
        total = part_s[rows(part_at, far, chunk), :].astype(F32)
        for d, copy in enumerate(copies):
            copy.wait_recv()
            total = total + far_in[d, pl.ds(before, chunk), :].astype(F32)
        mine = rows(whole_at, (core * lat_count + lat) * far_count + far, chunk)
        result[mine, :] = total.astype(BF16)
        copies = [send(result.at[mine], result.at[mine], along(d)) for d in range(1, far_count)]
        yield
        for copy in copies:
            copy.wait_recv()
        mine = rows(whole_at, core * lat_count + lat, part)
        copies = [send(result.at[mine], result.at[mine], across(d)) for d in range(1, lat_count)]
        yield
        for copy in copies:
            copy.wait_recv()
        mine = rows(whole_at, core, half)
        last = send(result.at[mine], result.at[mine], twin)
        yield
        last.wait_recv()

    pieces = [sum_piece(sum(chunks[:p]), chunk) for p, chunk in enumerate(chunks)]
    for piece in pieces:
        next(piece)
    rims = []
    at = 0
    for length, device in zip(rim_parts, rim_to):
        window = pl.ds(at, length)
        rims.append(send(rim_ref.at[window], rim_in.at[window], device))
        at += length
    for _ in range(5):
        for piece in pieces:
            next(piece)
    for copy in rims:
        copy.wait_recv()
    rim_out_ref[...] = rim_in[...]
    for piece in pieces:
        next(piece, None)

    for t in range(4 * C // LANES):
        narrow_s[:, t * LANES : (t + 1) * LANES] = result[t * C : (t + 1) * C, :].astype(F32)
    grad_qkv_ref[...] = narrow_s[:, : 3 * C].astype(BF16)
    grad_proj_ref[...] = narrow_s[:, 3 * C :].astype(BF16)
    for t in range(FF // LANES):
        grad_up_ref[:, t * LANES : (t + 1) * LANES] = result[UP_AT + t * C : UP_AT + (t + 1) * C, :]
    for t in range(FF // LANES):
        rows = slice(DOWN_AT + t * C, DOWN_AT + (t + 1) * C)
        grad_down_ref[:, t * LANES : (t + 1) * LANES] = result[rows, :]
    for copy in used:
        copy.wait_send()


def merge_patches(final, merge_weight):
    level_count, row_count, col_count, feat_count = final.shape
    grouped = final.reshape(level_count, row_count // 2, 2, col_count // 2, 2, feat_count)
    grouped = grouped.transpose(0, 1, 3, 2, 4, 5).reshape(-1, 4 * feat_count)
    center, inverse = center_of(grouped.astype(F32))
    merged = nn((center * inverse).astype(BF16), merge_weight).astype(BF16)
    return merged.reshape(level_count, row_count // 2, col_count // 2, 2 * feat_count)


def packed(cuts):
    flat = [cut.reshape(-1, cut.shape[-1]) for cut in cuts]
    lengths = [-(-cut.shape[0] // 16) * 16 for cut in flat]
    padded = [jnp.pad(cut, ((0, n - cut.shape[0]), (0, 0))) for cut, n in zip(flat, lengths)]

    def unpack(buffer):
        starts = [sum(lengths[:i]) for i in range(len(cuts))]
        return [
            buffer[at : at + part.shape[0]].reshape(cut.shape)
            for at, part, cut in zip(starts, flat, cuts)
        ]

    return jnp.concatenate(padded, axis=0), lengths, unpack


def per_device(
    tokens,
    cotangent,
    qkv_codes,
    proj_codes,
    up_codes,
    down_codes,
    bit_widths,
    quant_scales,
    bias_table,
    bias_index,
    merge_weight,
):
    level_count, row_count, col_count, feat_count = tokens.shape
    token_count = level_count * row_count * col_count
    window_rows = row_count // WLAT
    grid_shape = (level_count, row_count, col_count)
    lat_limit = lax.axis_size("lat") * row_count - LAT_PAD
    lat_index = lax.axis_index("lat")
    lat_start = lat_index * row_count - WLAT // 2
    row_ids = lat_index * row_count + jnp.arange(row_count, dtype=jnp.int32)
    row_mask = (row_ids < lat_limit)[None, :, None, None]

    both = jnp.concatenate([tokens, cotangent], axis=-1)
    both = jnp.where(row_mask, both, jnp.zeros_like(both))
    lon_count, lat_count = lax.axis_size("lon"), lax.axis_size("lat")
    rim_rows, rim_cols = WLAT // 2, WLON // 2
    pulled, lengths, unpack = packed(
        [both[:, :-rim_rows, rim_cols:], both[:, -rim_rows:, :rim_cols], both[:, -rim_rows:, rim_cols:]]
    )
    pair = bias_index.reshape(2, HALF, 2, HALF)
    index = jnp.concatenate([pair[0, :, 0], pair[1, :, 1]], axis=0)
    index = jnp.pad(index, ((0, 0), (0, LANES - HALF))).reshape(STEPS, -1)
    positions = bias_table.shape[-1]
    table_rows = window_rows * HEADS
    pieces, piece_rows = -(-positions // PIECE), -(-table_rows // 16) * 16
    table = bias_table.reshape(table_rows, positions)
    spare = ((0, piece_rows - table_rows), (0, pieces * PIECE - positions))
    table = jnp.pad(table, spare).reshape(piece_rows, pieces, PIECE).transpose(1, 0, 2)
    vmem = pl.BlockSpec(memory_space=pltpu.VMEM)
    smem = pl.BlockSpec(memory_space=pltpu.SMEM)
    codes = (qkv_codes, proj_codes, up_codes, down_codes.T)
    pulled, bias, *codes = pl.pallas_call(
        functools.partial(pull_kernel, lon_count, lat_count, lengths),
        out_shape=[
            jax.ShapeDtypeStruct(pulled.shape, BF16),
            jax.ShapeDtypeStruct((table_rows, WTOK, LANES), F32),
        ]
        + [jax.ShapeDtypeStruct(code.shape, jnp.int32) for code in codes],
        in_specs=[vmem] * 3 + [pl.BlockSpec(memory_space=pl.ANY)] * 4,
        out_specs=[vmem] * 6,
        scratch_shapes=[
            pltpu.VMEM(pulled.shape, BF16),
            pltpu.SemaphoreType.DMA((len(lengths),)),
            pltpu.SemaphoreType.DMA((len(lengths),)),
            pltpu.SemaphoreType.DMA((len(codes),)),
        ],
        compiler_params=pltpu.CompilerParams(
            collective_id=1, has_side_effects=True, vmem_limit_bytes=48 * 2**20
        ),
        name="pull_and_bias",
    )(pulled, index, table, *codes)
    got = unpack(pulled)
    upper = jnp.concatenate([got[2], got[1]], axis=2)
    lower = jnp.concatenate([got[0], both[:, :-rim_rows, :rim_cols]], axis=2)
    frame = jnp.concatenate([upper, lower], axis=1).reshape(token_count, 2 * feat_count)

    first_row = lat_start + WLAT * jnp.arange(window_rows, dtype=jnp.int32)
    edges = jnp.stack([-first_row * WLON, (lat_limit - first_row) * WLON], axis=1).reshape(-1)
    wide = jax.ShapeDtypeStruct((token_count, feat_count), BF16)
    chunk = -(-TOTAL_ROWS // (lon_count * lat_count * 16)) * 16
    total_rows = chunk * lon_count * lat_count
    final, grad, totals = pl.pallas_call(
        functools.partial(block_kernel, window_rows),
        out_shape=[wide, wide, jax.ShapeDtypeStruct((total_rows, LANES), BF16)],
        in_specs=[smem] + [vmem] * 7,
        out_specs=[vmem] * 3,
        scratch_shapes=[pltpu.VMEM((token_count, feat_count), F32)] * 4
        + [pltpu.VMEM((C, 4 * C), F32)],
        compiler_params=pltpu.CompilerParams(vmem_limit_bytes=48 * 2**20),
        name="block",
    )(
        jnp.concatenate([bit_widths, quant_scales, edges]),
        frame[:, :feat_count],
        frame[:, feat_count:],
        *codes,
        bias,
    )
    frame = jnp.concatenate([final, grad], axis=-1).reshape(grid_shape + (-1,))
    rim, lengths, unpack = packed(
        [frame[:, rim_rows:, :rim_cols], frame[:, :rim_rows, rim_cols:], frame[:, :rim_rows, :rim_cols]]
    )
    units = chunk // 16
    chunks = [16 * n for n in (units - units // 2, units // 2) if n]
    copies = 2 * (1 + lat_count - 1 + lon_count // 2 - 1) * len(chunks) + len(lengths)
    half = total_rows // 2
    part = half // lat_count
    *grads, rim = pl.pallas_call(
        functools.partial(reduce_kernel, lon_count, lat_count, lengths, chunks),
        out_shape=[
            jax.ShapeDtypeStruct((C, 3 * C), BF16),
            jax.ShapeDtypeStruct((C, C), BF16),
            jax.ShapeDtypeStruct((C, FF), BF16),
            jax.ShapeDtypeStruct((C, FF), BF16),
            jax.ShapeDtypeStruct(rim.shape, BF16),
        ],
        in_specs=[vmem] * 2,
        out_specs=[vmem] * 5,
        scratch_shapes=[
            pltpu.VMEM((half, LANES), BF16),
            pltpu.VMEM((lat_count - 1, part, LANES), BF16),
            pltpu.VMEM((lon_count // 2 - 1, chunk, LANES), BF16),
            pltpu.VMEM((half, LANES), BF16),
            pltpu.VMEM((part, LANES), BF16),
            pltpu.VMEM((total_rows, LANES), BF16),
            pltpu.VMEM(rim.shape, BF16),
            pltpu.VMEM((C, 4 * C), F32),
            pltpu.SemaphoreType.DMA((copies,)),
            pltpu.SemaphoreType.DMA((copies,)),
        ],
        compiler_params=pltpu.CompilerParams(
            collective_id=0, has_side_effects=True, vmem_limit_bytes=48 * 2**20
        ),
        name="reduce_and_push",
    )(totals, rim)
    got = unpack(rim)
    upper = jnp.concatenate([frame[:, rim_rows:, rim_cols:], got[0]], axis=2)
    lower = jnp.concatenate([got[1], got[2]], axis=2)
    owned = jnp.concatenate([upper, lower], axis=1)
    owned = jnp.where(row_mask, owned, jnp.zeros_like(owned))
    merged = merge_patches(owned[..., :feat_count], merge_weight)
    return (merged, owned[..., feat_count:]) + tuple(grads[:3]) + (grads[3].T,)


def solution(mesh):
    split = P(None, "lat", "lon", None)
    placed = (split, split, P(), P(), P(), P(), P(), P(), P("lat", None, None, None), P(), P())
    return jax.shard_map(
        per_device,
        mesh=mesh,
        in_specs=placed,
        out_specs=(split, split, P(), P(), P(), P()),
        check_vma=False,
    )
```

```python
import functools
import math

import jax
import jax.numpy as jnp
from jax import lax
from jax.experimental import pallas as pl
from jax.experimental.pallas import tpu as pltpu
from jax.sharding import PartitionSpec as P

C = 192
HEADS = 6
FF = 768
HEAD_DIM = 32
WLAT = 6
WLON = 12
LAT_PAD = 11
WTOK = 144
HALF = 72
LANES = 128
PIECE = 256
STEPS = 12
EPSILON = 1e-05
MASKED = -1000000000.0
UP_AT = 6 * C
DOWN_AT = 12 * C
TOTAL_ROWS = 18 * C
F32 = jnp.float32
BF16 = jnp.bfloat16


def nn(left, right):
    return lax.dot_general(left, right, (((1,), (0,)), ((), ())), preferred_element_type=F32)


def nt(left, right):
    return lax.dot_general(left, right, (((1,), (1,)), ((), ())), preferred_element_type=F32)


def tn(left, right):
    return lax.dot_general(left, right, (((0,), (0,)), ((), ())), preferred_element_type=F32)


def neighbours(lon_count, lat_count):
    lon, lat = lax.axis_index("lon"), lax.axis_index("lat")
    west, east = lax.rem(lon + lon_count - 1, lon_count), lax.rem(lon + 1, lon_count)
    north, south = lax.rem(lat + lat_count - 1, lat_count), lax.rem(lat + 1, lat_count)
    behind = [{"lon": west, "lat": lat}, {"lon": lon, "lat": north}, {"lon": west, "lat": north}]
    ahead = [{"lon": east, "lat": lat}, {"lon": lon, "lat": south}, {"lon": east, "lat": south}]
    return behind, ahead


def greet(devices):
    barrier = pltpu.get_barrier_semaphore()
    for device in devices:
        pl.semaphore_signal(barrier, inc=1, device_id=device, device_id_type=pl.DeviceIdType.MESH)
    pl.semaphore_wait(barrier, len(devices))


def pull_kernel(
    lon_count,
    lat_count,
    rim_parts,
    rim_ref,
    index_ref,
    table_ref,
    rim_out_ref,
    bias_ref,
    rim_in,
    sends,
    receives,
):
    behind, ahead = neighbours(lon_count, lat_count)
    greet(behind + ahead)
    copies = []
    at = 0
    for slot, (length, device) in enumerate(zip(rim_parts, ahead)):
        copy = pltpu.make_async_remote_copy(
            src_ref=rim_ref.at[pl.ds(at, length)],
            dst_ref=rim_in.at[pl.ds(at, length)],
            send_sem=sends.at[slot],
            recv_sem=receives.at[slot],
            device_id=device,
            device_id_type=pl.DeviceIdType.MESH,
        )
        copy.start()
        copies.append(copy)
        at += length

    steps, width = index_ref.shape
    table_rows = bias_ref.shape[0]
    pieces, piece_rows, piece = table_ref.shape
    tables = table_ref[...].reshape(pieces * piece_rows, piece)
    inside = lax.broadcasted_iota(jnp.int32, (piece, width), 0)

    def one_step(step, carry):
        index = index_ref[pl.ds(step, 1), :]
        low = jnp.bitwise_and(index, piece - 1)
        high = jnp.right_shift(index, piece.bit_length() - 1)
        chosen = jnp.where(inside == low, 1.0, 0.0).astype(BF16)
        found = nn(tables, chosen)
        total = found[:piece_rows]
        for p in range(1, pieces):
            total = jnp.where(high == p, found[p * piece_rows : (p + 1) * piece_rows], total)
        for i in range(width // LANES):
            for r in range(table_rows):
                row = total[r : r + 1, i * LANES : (i + 1) * LANES]
                bias_ref[r, pl.ds(step * (width // LANES) + i, 1), :] = row
        return carry

    lax.fori_loop(0, steps, one_step, 0)
    for copy in copies:
        copy.wait_recv()
    rim_out_ref[...] = rim_in[...]
    for copy in copies:
        copy.wait_send()


def center_of(values):
    center = values - jnp.mean(values, axis=-1, keepdims=True)
    spread = jnp.mean(center * center, axis=-1, keepdims=True)
    return center, lax.rsqrt(spread + EPSILON)


def norm_back(center, scale, upstream):
    inner = jnp.mean(upstream * center, axis=-1, keepdims=True)
    outer = jnp.mean(upstream, axis=-1, keepdims=True)
    return scale * (upstream - outer - center * (scale * scale * inner))


def block_kernel(
    window_rows,
    scalars_ref,
    start_ref,
    d_out_ref,
    qkv_ref,
    bias_ref,
    proj_ref,
    up_ref,
    down_ref,
    final_ref,
    grad_ref,
    totals_ref,
    heads_s,
    dq_s,
    dk_s,
    dv_s,
    narrow_s,
):
    def dequant(codes, layer, fan_in):
        largest = jnp.left_shift(jnp.int32(1), scalars_ref[layer] - 1) - 1
        scale = jnp.full((1, codes.shape[1]), scalars_ref[4 + layer].astype(F32), F32)
        factor = math.sqrt(C / fan_in) / scale
        return (jnp.clip(codes, -largest, largest).astype(F32) * factor).astype(BF16)

    start = start_ref[...].astype(F32)
    center, inverse = center_of(start)
    normed = (center * inverse).astype(BF16)
    w_q = dequant(qkv_ref[:, :C], 0, C)
    w_k = dequant(qkv_ref[:, C : 2 * C], 0, C)
    w_v = dequant(qkv_ref[:, 2 * C :], 0, C)
    q = nn(normed, w_q).astype(BF16)
    k = nn(normed, w_k).astype(BF16)
    v = nn(normed, w_v).astype(BF16)

    lane = lax.broadcasted_iota(jnp.int32, (HALF, C), 1)
    head_masks = [(lane >= h * HEAD_DIM) & (lane < (h + 1) * HEAD_DIM) for h in range(HEADS)]

    def stack(values):
        wide = values.astype(F32)
        return jnp.concatenate([jnp.where(m, wide, 0.0) for m in head_masks], axis=0).astype(BF16)

    def unstack(values):
        total = jnp.zeros((HALF, C), F32)
        for h, m in enumerate(head_masks):
            total = jnp.where(m, values[h * HALF : (h + 1) * HALF], total)
        return total

    keys = lax.broadcasted_iota(jnp.int32, (HEADS * HALF, HALF), 1)
    blocks = start.shape[0] // HALF
    saved = []
    for b in range(blocks):
        level, a = b // window_rows, b % window_rows
        part = slice(b * HALF, (b + 1) * HALF)
        stacked_q = stack(q[part])
        bias = bias_ref[a * HEADS : (a + 1) * HEADS, (1 - level) * HALF : (2 - level) * HALF, :]
        bias = bias.reshape(HEADS * HALF, LANES)[:, :HALF]
        scores = nt(stacked_q, k[part]) * HEAD_DIM ** (-0.5) + bias
        allowed = (keys >= scalars_ref[8 + 2 * a]) & (keys < scalars_ref[9 + 2 * a])
        scores = jnp.where(allowed, scores, MASKED)
        weights = jnp.exp(scores - jnp.max(scores, axis=-1, keepdims=True))
        weights = weights / jnp.sum(weights, axis=-1, keepdims=True)
        saved.append((stacked_q, weights, allowed))
        heads_s[part, :] = unstack(nn(weights.astype(BF16), v[part]))

    heads = heads_s[...].astype(BF16)
    w_proj = dequant(proj_ref[...], 1, C)
    resid = (start + nn(heads, w_proj)).astype(BF16)
    center_two, inverse_two = center_of(resid.astype(F32))
    normed_two = (center_two * inverse_two).astype(BF16)
    w_up = dequant(up_ref[...], 2, C)
    w_down_t = dequant(down_ref[...], 3, FF)
    pre = nn(normed_two, w_up)
    cubic = math.sqrt(2 / math.pi)
    square = pre * pre
    bent = jnp.tanh(cubic * (pre + 0.044715 * square * pre))
    hidden = (0.5 * pre * (1.0 + bent)).astype(BF16)
    final_ref[...] = (resid.astype(F32) + nt(hidden, w_down_t)).astype(BF16)
    d_out = d_out_ref[...]
    down_total = tn(d_out, hidden).astype(BF16)
    for t in range(FF // LANES):
        rows = slice(DOWN_AT + t * C, DOWN_AT + (t + 1) * C)
        totals_ref[rows, :] = down_total[:, t * LANES : (t + 1) * LANES]
    d_hidden = nn(d_out, w_down_t).astype(BF16).astype(F32)
    slope = 0.5 * (1.0 + bent) + 0.5 * pre * (1.0 - bent * bent) * cubic * (
        1.0 + 3 * 0.044715 * square
    )
    d_pre = (slope * d_hidden).astype(BF16)
    up_total = tn(normed_two, d_pre).astype(BF16)
    for t in range(FF // LANES):
        totals_ref[UP_AT + t * C : UP_AT + (t + 1) * C, :] = up_total[:, t * LANES : (t + 1) * LANES]
    d_normed_two = nt(d_pre, w_up).astype(BF16).astype(F32)
    d_resid = (d_out.astype(F32) + norm_back(center_two, inverse_two, d_normed_two)).astype(BF16)
    narrow_s[:, 3 * C :] = tn(heads, d_resid)
    d_heads = nt(d_resid, w_proj).astype(BF16)

    for b in range(blocks):
        part = slice(b * HALF, (b + 1) * HALF)
        stacked_q, weights, allowed = saved[b]
        d_stacked = stack(d_heads[part])
        d_weights = nt(d_stacked, v[part]).astype(BF16).astype(F32)
        dv_s[part, :] = tn(weights.astype(BF16), d_stacked)
        inner = jnp.sum(weights * d_weights, axis=-1, keepdims=True)
        d_scores = jnp.where(allowed, weights * (d_weights - inner), 0.0)
        d_scores = (d_scores * HEAD_DIM ** (-0.5)).astype(BF16)
        dq_s[part, :] = unstack(nn(d_scores, k[part]))
        dk_s[part, :] = tn(d_scores, stacked_q)

    dq = dq_s[...].astype(BF16)
    dk = dk_s[...].astype(BF16)
    dv = dv_s[...].astype(BF16)
    narrow_s[:, :C] = tn(normed, dq)
    narrow_s[:, C : 2 * C] = tn(normed, dk)
    narrow_s[:, 2 * C : 3 * C] = tn(normed, dv)
    for t in range(4 * C // LANES):
        tile = narrow_s[:, t * LANES : (t + 1) * LANES]
        totals_ref[t * C : (t + 1) * C, :] = tile.astype(BF16)
    spare = totals_ref.shape[0] - TOTAL_ROWS
    if spare:
        totals_ref[TOTAL_ROWS:, :] = jnp.zeros((spare, LANES), BF16)
    d_normed = (nt(dq, w_q) + nt(dk, w_k) + nt(dv, w_v)).astype(BF16).astype(F32)
    grad_ref[...] = (d_resid.astype(F32) + norm_back(center, inverse, d_normed)).astype(BF16)


def reduce_kernel(
    lon_count,
    lat_count,
    rim_parts,
    chunks,
    totals_ref,
    rim_ref,
    grad_qkv_ref,
    grad_proj_ref,
    grad_up_ref,
    grad_down_ref,
    rim_out_ref,
    core_in,
    lat_in,
    far_in,
    half_s,
    part_s,
    result,
    rim_in,
    narrow_s,
    sends,
    receives,
):
    lon, lat = lax.axis_index("lon"), lax.axis_index("lat")
    core, far, far_count = lax.rem(lon, 2), lon // 2, lon_count // 2
    def across(distance):
        return {"lon": lon, "lat": lax.rem(lat + distance + lat_count, lat_count)}

    def along(distance):
        other = lax.rem(far + distance + far_count, far_count)
        return {"lon": other * 2 + core, "lat": lat}

    twin = {"lon": far * 2 + 1 - core, "lat": lat}
    rim_to, rim_from = neighbours(lon_count, lat_count)
    greeted = [twin] + [across(d) for d in range(1, lat_count)]
    greeted += [along(d) for d in range(1, far_count)] + rim_to + rim_from
    greet(greeted)

    used = []

    def send(source, target, device):
        slot = len(used)
        copy = pltpu.make_async_remote_copy(
            src_ref=source,
            dst_ref=target,
            send_sem=sends.at[slot],
            recv_sem=receives.at[slot],
            device_id=device,
            device_id_type=pl.DeviceIdType.MESH,
        )
        copy.start()
        used.append(copy)
        return copy

    def sum_piece(before, chunk):
        part = chunk * far_count
        half = part * lat_count
        part_at, half_at, whole_at = before * far_count, before * far_count * lat_count, 0
        whole_at = 2 * half_at

        def rows(start, index, size):
            return pl.ds(pl.multiple_of(start + index * size, 16), size)

        arriving = core_in.at[pl.ds(half_at, half)]
        first = send(totals_ref.at[rows(whole_at, 1 - core, half)], arriving, twin)
        yield
        first.wait_recv()
        total = totals_ref[rows(whole_at, core, half), :].astype(F32)
        total = total + core_in[pl.ds(half_at, half), :].astype(F32)
        half_s[pl.ds(half_at, half), :] = total.astype(BF16)
        copies = []
        for d in range(1, lat_count):
            source = half_s.at[rows(half_at, lax.rem(lat + d, lat_count), part)]
            copies.append(send(source, lat_in.at[d - 1, pl.ds(part_at, part)], across(d)))
        yield
        total = half_s[rows(half_at, lat, part), :].astype(F32)
        for d, copy in enumerate(copies):
            copy.wait_recv()
            total = total + lat_in[d, pl.ds(part_at, part), :].astype(F32)
        part_s[pl.ds(part_at, part), :] = total.astype(BF16)
        copies = []
        for d in range(1, far_count):
            source = part_s.at[rows(part_at, lax.rem(far + d, far_count), chunk)]
            copies.append(send(source, far_in.at[d - 1, pl.ds(before, chunk)], along(d)))
        yield
        total = part_s[rows(part_at, far, chunk), :].astype(F32)
        for d, copy in enumerate(copies):
            copy.wait_recv()
            total = total + far_in[d, pl.ds(before, chunk), :].astype(F32)
        mine = rows(whole_at, (core * lat_count + lat) * far_count + far, chunk)
        result[mine, :] = total.astype(BF16)
        copies = [send(result.at[mine], result.at[mine], along(d)) for d in range(1, far_count)]
        yield
        for copy in copies:
            copy.wait_recv()
        mine = rows(whole_at, core * lat_count + lat, part)
        copies = [send(result.at[mine], result.at[mine], across(d)) for d in range(1, lat_count)]
        yield
        for copy in copies:
            copy.wait_recv()
        mine = rows(whole_at, core, half)
        last = send(result.at[mine], result.at[mine], twin)
        yield
        last.wait_recv()

    pieces = [sum_piece(sum(chunks[:p]), chunk) for p, chunk in enumerate(chunks)]
    for piece in pieces:
        next(piece)
    rims = []
    at = 0
    for length, device in zip(rim_parts, rim_to):
        window = pl.ds(at, length)
        rims.append(send(rim_ref.at[window], rim_in.at[window], device))
        at += length
    for _ in range(5):
        for piece in pieces:
            next(piece)
    for copy in rims:
        copy.wait_recv()
    rim_out_ref[...] = rim_in[...]
    for piece in pieces:
        next(piece, None)

    for t in range(4 * C // LANES):
        narrow_s[:, t * LANES : (t + 1) * LANES] = result[t * C : (t + 1) * C, :].astype(F32)
    grad_qkv_ref[...] = narrow_s[:, : 3 * C].astype(BF16)
    grad_proj_ref[...] = narrow_s[:, 3 * C :].astype(BF16)
    for t in range(FF // LANES):
        grad_up_ref[:, t * LANES : (t + 1) * LANES] = result[UP_AT + t * C : UP_AT + (t + 1) * C, :]
    for t in range(FF // LANES):
        rows = slice(DOWN_AT + t * C, DOWN_AT + (t + 1) * C)
        grad_down_ref[:, t * LANES : (t + 1) * LANES] = result[rows, :]
    for copy in used:
        copy.wait_send()


def merge_patches(final, merge_weight):
    level_count, row_count, col_count, feat_count = final.shape
    grouped = final.reshape(level_count, row_count // 2, 2, col_count // 2, 2, feat_count)
    grouped = grouped.transpose(0, 1, 3, 2, 4, 5).reshape(-1, 4 * feat_count)
    center, inverse = center_of(grouped.astype(F32))
    merged = nn((center * inverse).astype(BF16), merge_weight).astype(BF16)
    return merged.reshape(level_count, row_count // 2, col_count // 2, 2 * feat_count)


def packed(cuts):
    flat = [cut.reshape(-1, cut.shape[-1]) for cut in cuts]
    lengths = [-(-cut.shape[0] // 16) * 16 for cut in flat]
    padded = [jnp.pad(cut, ((0, n - cut.shape[0]), (0, 0))) for cut, n in zip(flat, lengths)]

    def unpack(buffer):
        starts = [sum(lengths[:i]) for i in range(len(cuts))]
        return [
            buffer[at : at + part.shape[0]].reshape(cut.shape)
            for at, part, cut in zip(starts, flat, cuts)
        ]

    return jnp.concatenate(padded, axis=0), lengths, unpack


def per_device(
    tokens,
    cotangent,
    qkv_codes,
    proj_codes,
    up_codes,
    down_codes,
    bit_widths,
    quant_scales,
    bias_table,
    bias_index,
    merge_weight,
):
    level_count, row_count, col_count, feat_count = tokens.shape
    token_count = level_count * row_count * col_count
    window_rows = row_count // WLAT
    grid_shape = (level_count, row_count, col_count)
    lat_limit = lax.axis_size("lat") * row_count - LAT_PAD
    lat_index = lax.axis_index("lat")
    lat_start = lat_index * row_count - WLAT // 2
    row_ids = lat_index * row_count + jnp.arange(row_count, dtype=jnp.int32)
    row_mask = (row_ids < lat_limit)[None, :, None, None]

    both = jnp.concatenate([tokens, cotangent], axis=-1)
    both = jnp.where(row_mask, both, jnp.zeros_like(both))
    lon_count, lat_count = lax.axis_size("lon"), lax.axis_size("lat")
    rim_rows, rim_cols = WLAT // 2, WLON // 2
    pulled, lengths, unpack = packed(
        [both[:, :-rim_rows, rim_cols:], both[:, -rim_rows:, :rim_cols], both[:, -rim_rows:, rim_cols:]]
    )
    pair = bias_index.reshape(2, HALF, 2, HALF)
    index = jnp.concatenate([pair[0, :, 0], pair[1, :, 1]], axis=0)
    index = jnp.pad(index, ((0, 0), (0, LANES - HALF))).reshape(STEPS, -1)
    positions = bias_table.shape[-1]
    table_rows = window_rows * HEADS
    pieces, piece_rows = -(-positions // PIECE), -(-table_rows // 16) * 16
    table = bias_table.reshape(table_rows, positions)
    spare = ((0, piece_rows - table_rows), (0, pieces * PIECE - positions))
    table = jnp.pad(table, spare).reshape(piece_rows, pieces, PIECE).transpose(1, 0, 2)
    vmem = pl.BlockSpec(memory_space=pltpu.VMEM)
    smem = pl.BlockSpec(memory_space=pltpu.SMEM)
    pulled, bias = pl.pallas_call(
        functools.partial(pull_kernel, lon_count, lat_count, lengths),
        out_shape=[
            jax.ShapeDtypeStruct(pulled.shape, BF16),
            jax.ShapeDtypeStruct((table_rows, WTOK, LANES), F32),
        ],
        in_specs=[vmem] * 3,
        out_specs=[vmem] * 2,
        scratch_shapes=[
            pltpu.VMEM(pulled.shape, BF16),
            pltpu.SemaphoreType.DMA((len(lengths),)),
            pltpu.SemaphoreType.DMA((len(lengths),)),
        ],
        compiler_params=pltpu.CompilerParams(
            collective_id=1, has_side_effects=True, vmem_limit_bytes=32 * 2**20
        ),
        cost_estimate=pl.CostEstimate(
            flops=2 * table.size * index.size, bytes_accessed=20 * 10**6, transcendentals=0
        ),
        name="pull_and_bias",
    )(pulled, index, table)
    got = unpack(pulled)
    upper = jnp.concatenate([got[2], got[1]], axis=2)
    lower = jnp.concatenate([got[0], both[:, :-rim_rows, :rim_cols]], axis=2)
    frame = jnp.concatenate([upper, lower], axis=1).reshape(token_count, 2 * feat_count)

    first_row = lat_start + WLAT * jnp.arange(window_rows, dtype=jnp.int32)
    edges = jnp.stack([-first_row * WLON, (lat_limit - first_row) * WLON], axis=1).reshape(-1)
    operands = (qkv_codes, bias, proj_codes, up_codes, down_codes.T)
    wide = jax.ShapeDtypeStruct((token_count, feat_count), BF16)
    chunk = -(-TOTAL_ROWS // (lon_count * lat_count * 16)) * 16
    total_rows = chunk * lon_count * lat_count
    final, grad, totals = pl.pallas_call(
        functools.partial(block_kernel, window_rows),
        out_shape=[wide, wide, jax.ShapeDtypeStruct((total_rows, LANES), BF16)],
        in_specs=[smem] + [vmem] * 7,
        out_specs=[vmem] * 3,
        scratch_shapes=[pltpu.VMEM((token_count, feat_count), F32)] * 4
        + [pltpu.VMEM((C, 4 * C), F32)],
        compiler_params=pltpu.CompilerParams(vmem_limit_bytes=32 * 2**20),
        cost_estimate=pl.CostEstimate(
            flops=2 * 10**9, bytes_accessed=20 * 10**6, transcendentals=10**6
        ),
        name="block",
    )(
        jnp.concatenate([bit_widths, quant_scales, edges]),
        frame[:, :feat_count],
        frame[:, feat_count:],
        *operands,
    )
    frame = jnp.concatenate([final, grad], axis=-1).reshape(grid_shape + (-1,))
    rim, lengths, unpack = packed(
        [frame[:, rim_rows:, :rim_cols], frame[:, :rim_rows, rim_cols:], frame[:, :rim_rows, :rim_cols]]
    )
    units = chunk // 16
    chunks = [16 * n for n in (units - units // 2, units // 2) if n]
    copies = 2 * (1 + lat_count - 1 + lon_count // 2 - 1) * len(chunks) + len(lengths)
    half = total_rows // 2
    part = half // lat_count
    *grads, rim = pl.pallas_call(
        functools.partial(reduce_kernel, lon_count, lat_count, lengths, chunks),
        out_shape=[
            jax.ShapeDtypeStruct((C, 3 * C), BF16),
            jax.ShapeDtypeStruct((C, C), BF16),
            jax.ShapeDtypeStruct((C, FF), BF16),
            jax.ShapeDtypeStruct((C, FF), BF16),
            jax.ShapeDtypeStruct(rim.shape, BF16),
        ],
        in_specs=[vmem] * 2,
        out_specs=[vmem] * 5,
        scratch_shapes=[
            pltpu.VMEM((half, LANES), BF16),
            pltpu.VMEM((lat_count - 1, part, LANES), BF16),
            pltpu.VMEM((lon_count // 2 - 1, chunk, LANES), BF16),
            pltpu.VMEM((half, LANES), BF16),
            pltpu.VMEM((part, LANES), BF16),
            pltpu.VMEM((total_rows, LANES), BF16),
            pltpu.VMEM(rim.shape, BF16),
            pltpu.VMEM((C, 4 * C), F32),
            pltpu.SemaphoreType.DMA((copies,)),
            pltpu.SemaphoreType.DMA((copies,)),
        ],
        compiler_params=pltpu.CompilerParams(
            collective_id=0, has_side_effects=True, vmem_limit_bytes=48 * 2**20
        ),
        cost_estimate=pl.CostEstimate(
            flops=10**7, bytes_accessed=60 * 10**6, transcendentals=0
        ),
        name="reduce_and_push",
    )(totals, rim)
    got = unpack(rim)
    upper = jnp.concatenate([frame[:, rim_rows:, rim_cols:], got[0]], axis=2)
    lower = jnp.concatenate([got[1], got[2]], axis=2)
    owned = jnp.concatenate([upper, lower], axis=1)
    owned = jnp.where(row_mask, owned, jnp.zeros_like(owned))
    merged = merge_patches(owned[..., :feat_count], merge_weight)
    return (merged, owned[..., feat_count:]) + tuple(grads[:3]) + (grads[3].T,)


def solution(mesh):
    split = P(None, "lat", "lon", None)
    placed = (split, split, P(), P(), P(), P(), P(), P(), P("lat", None, None, None), P(), P())
    return jax.shard_map(
        per_device,
        mesh=mesh,
        in_specs=placed,
        out_specs=(split, split, P(), P(), P(), P()),
        check_vma=False,
    )
```

```python
import functools
import math

import jax
import jax.numpy as jnp
from jax import lax
from jax.experimental import pallas as pl
from jax.experimental.pallas import tpu as pltpu
from jax.sharding import PartitionSpec as P

C = 192
HEADS = 6
FF = 768
HEAD_DIM = 32
WLAT = 6
WLON = 12
LAT_PAD = 11
WTOK = 144
HALF = 72
LANES = 128
PIECE = 256
STEPS = 7
TAIL = 16
EPSILON = 1e-05
MASKED = -1000000000.0
UP_AT = 6 * C
DOWN_AT = 12 * C
TOTAL_ROWS = 18 * C
F32 = jnp.float32
BF16 = jnp.bfloat16


def nn(left, right):
    return lax.dot_general(left, right, (((1,), (0,)), ((), ())), preferred_element_type=F32)


def nt(left, right):
    return lax.dot_general(left, right, (((1,), (1,)), ((), ())), preferred_element_type=F32)


def tn(left, right):
    return lax.dot_general(left, right, (((0,), (0,)), ((), ())), preferred_element_type=F32)


def neighbours(lon_count, lat_count):
    lon, lat = lax.axis_index("lon"), lax.axis_index("lat")
    west, east = lax.rem(lon + lon_count - 1, lon_count), lax.rem(lon + 1, lon_count)
    north, south = lax.rem(lat + lat_count - 1, lat_count), lax.rem(lat + 1, lat_count)
    behind = [{"lon": west, "lat": lat}, {"lon": lon, "lat": north}, {"lon": west, "lat": north}]
    ahead = [{"lon": east, "lat": lat}, {"lon": lon, "lat": south}, {"lon": east, "lat": south}]
    return behind, ahead


def greet(devices):
    barrier = pltpu.get_barrier_semaphore()
    for device in devices:
        pl.semaphore_signal(barrier, inc=1, device_id=device, device_id_type=pl.DeviceIdType.MESH)
    pl.semaphore_wait(barrier, len(devices))


def pull_kernel(
    lon_count,
    lat_count,
    rim_parts,
    rim_ref,
    index_ref,
    table_ref,
    rim_out_ref,
    bias_ref,
    rim_in,
    sends,
    receives,
):
    behind, ahead = neighbours(lon_count, lat_count)
    greet(behind + ahead)
    copies = []
    at = 0
    for slot, (length, device) in enumerate(zip(rim_parts, ahead)):
        copy = pltpu.make_async_remote_copy(
            src_ref=rim_ref.at[pl.ds(at, length)],
            dst_ref=rim_in.at[pl.ds(at, length)],
            send_sem=sends.at[slot],
            recv_sem=receives.at[slot],
            device_id=device,
            device_id_type=pl.DeviceIdType.MESH,
        )
        copy.start()
        copies.append(copy)
        at += length

    steps, width = index_ref.shape
    table_rows = bias_ref.shape[0]
    pieces, piece_rows, piece = table_ref.shape
    tables = table_ref[...].reshape(pieces * piece_rows, piece)
    inside = lax.broadcasted_iota(jnp.int32, (piece, width), 0)

    tiles = width // LANES

    def values_of(index):
        low = jnp.bitwise_and(index, piece - 1)
        high = jnp.right_shift(index, piece.bit_length() - 1)
        chosen = jnp.where(inside == low, 1.0, 0.0).astype(BF16)
        found = nn(tables, chosen)
        total = found[:piece_rows]
        for p in range(1, pieces):
            total = jnp.where(high == p, found[p * piece_rows : (p + 1) * piece_rows], total)
        return total

    def one_step(step, carry):
        total = values_of(index_ref[pl.ds(step, 1), :])
        for i in range(tiles):
            for r in range(table_rows):
                row = total[r : r + 1, i * LANES : (i + 1) * LANES]
                bias_ref[r, pl.ds(step * tiles + i, 1), :] = row
        return carry

    lax.fori_loop(0, steps - 1, one_step, 0)
    total = values_of(index_ref[steps - 1 : steps, :])
    group = LANES // TAIL
    for q in range(HALF):
        tile = total[:, q // group * LANES : (q // group + 1) * LANES]
        if q % group:
            tile = pltpu.roll(tile, LANES - q % group * TAIL, 1)
        for r in range(table_rows):
            bias_ref[r, HALF + q : HALF + q + 1, :] = tile[r : r + 1]
    for copy in copies:
        copy.wait_recv()
    rim_out_ref[...] = rim_in[...]
    for copy in copies:
        copy.wait_send()


def center_of(values):
    center = values - jnp.mean(values, axis=-1, keepdims=True)
    spread = jnp.mean(center * center, axis=-1, keepdims=True)
    return center, lax.rsqrt(spread + EPSILON)


def norm_back(center, scale, upstream):
    inner = jnp.mean(upstream * center, axis=-1, keepdims=True)
    outer = jnp.mean(upstream, axis=-1, keepdims=True)
    return scale * (upstream - outer - center * (scale * scale * inner))


def block_kernel(
    window_rows,
    scalars_ref,
    start_ref,
    d_out_ref,
    qkv_ref,
    bias_ref,
    proj_ref,
    up_ref,
    down_ref,
    final_ref,
    grad_ref,
    totals_ref,
    heads_s,
    dq_s,
    dk_s,
    dv_s,
    narrow_s,
):
    def dequant(codes, layer, fan_in):
        largest = jnp.left_shift(jnp.int32(1), scalars_ref[layer] - 1) - 1
        scale = jnp.full((1, codes.shape[1]), scalars_ref[4 + layer].astype(F32), F32)
        factor = math.sqrt(C / fan_in) / scale
        return (jnp.clip(codes, -largest, largest).astype(F32) * factor).astype(BF16)

    start = start_ref[...].astype(F32)
    center, inverse = center_of(start)
    normed = (center * inverse).astype(BF16)
    w_q = dequant(qkv_ref[:, :C], 0, C)
    w_k = dequant(qkv_ref[:, C : 2 * C], 0, C)
    w_v = dequant(qkv_ref[:, 2 * C :], 0, C)
    q = nn(normed, w_q).astype(BF16)
    k = nn(normed, w_k).astype(BF16)
    v = nn(normed, w_v).astype(BF16)

    lane = lax.broadcasted_iota(jnp.int32, (HALF, C), 1)
    head_masks = [(lane >= h * HEAD_DIM) & (lane < (h + 1) * HEAD_DIM) for h in range(HEADS)]

    def stack(values):
        wide = values.astype(F32)
        return jnp.concatenate([jnp.where(m, wide, 0.0) for m in head_masks], axis=0).astype(BF16)

    def unstack(values):
        total = jnp.zeros((HALF, C), F32)
        for h, m in enumerate(head_masks):
            total = jnp.where(m, values[h * HALF : (h + 1) * HALF], total)
        return total

    keys = lax.broadcasted_iota(jnp.int32, (HEADS * HALF, HALF), 1)
    blocks = start.shape[0] // HALF
    saved = []
    for b in range(blocks):
        level, a = b // window_rows, b % window_rows
        part = slice(b * HALF, (b + 1) * HALF)
        stacked_q = stack(q[part])
        table = bias_ref[a * HEADS : (a + 1) * HEADS, :, :]
        wide = table[:, :HALF, :].reshape(HEADS * HALF, LANES)
        tail = table[:, HALF:, :].reshape(HEADS * HALF, LANES)
        wide_at, tail_at = (1 - level) * (LANES // 2), (1 - level) * (TAIL // 2)
        bias = jnp.concatenate(
            [wide[:, wide_at : wide_at + LANES // 2], tail[:, tail_at : tail_at + TAIL // 2]], axis=1
        )
        scores = nt(stacked_q, k[part]) * HEAD_DIM ** (-0.5) + bias
        allowed = (keys >= scalars_ref[8 + 2 * a]) & (keys < scalars_ref[9 + 2 * a])
        scores = jnp.where(allowed, scores, MASKED)
        weights = jnp.exp(scores - jnp.max(scores, axis=-1, keepdims=True))
        weights = weights / jnp.sum(weights, axis=-1, keepdims=True)
        saved.append((stacked_q, weights, allowed))
        heads_s[part, :] = unstack(nn(weights.astype(BF16), v[part]))

    heads = heads_s[...].astype(BF16)
    w_proj = dequant(proj_ref[...], 1, C)
    resid = (start + nn(heads, w_proj)).astype(BF16)
    center_two, inverse_two = center_of(resid.astype(F32))
    normed_two = (center_two * inverse_two).astype(BF16)
    w_up = dequant(up_ref[...], 2, C)
    w_down_t = dequant(down_ref[...], 3, FF)
    pre = nn(normed_two, w_up)
    cubic = math.sqrt(2 / math.pi)
    square = pre * pre
    bent = jnp.tanh(cubic * (pre + 0.044715 * square * pre))
    hidden = (0.5 * pre * (1.0 + bent)).astype(BF16)
    final_ref[...] = (resid.astype(F32) + nt(hidden, w_down_t)).astype(BF16)
    d_out = d_out_ref[...]
    down_total = tn(d_out, hidden).astype(BF16)
    for t in range(FF // LANES):
        rows = slice(DOWN_AT + t * C, DOWN_AT + (t + 1) * C)
        totals_ref[rows, :] = down_total[:, t * LANES : (t + 1) * LANES]
    d_hidden = nn(d_out, w_down_t).astype(BF16).astype(F32)
    slope = 0.5 * (1.0 + bent) + 0.5 * pre * (1.0 - bent * bent) * cubic * (
        1.0 + 3 * 0.044715 * square
    )
    d_pre = (slope * d_hidden).astype(BF16)
    up_total = tn(normed_two, d_pre).astype(BF16)
    for t in range(FF // LANES):
        totals_ref[UP_AT + t * C : UP_AT + (t + 1) * C, :] = up_total[:, t * LANES : (t + 1) * LANES]
    d_normed_two = nt(d_pre, w_up).astype(BF16).astype(F32)
    d_resid = (d_out.astype(F32) + norm_back(center_two, inverse_two, d_normed_two)).astype(BF16)
    narrow_s[:, 3 * C :] = tn(heads, d_resid)
    d_heads = nt(d_resid, w_proj).astype(BF16)

    for b in range(blocks):
        part = slice(b * HALF, (b + 1) * HALF)
        stacked_q, weights, allowed = saved[b]
        d_stacked = stack(d_heads[part])
        d_weights = nt(d_stacked, v[part]).astype(BF16).astype(F32)
        dv_s[part, :] = tn(weights.astype(BF16), d_stacked)
        inner = jnp.sum(weights * d_weights, axis=-1, keepdims=True)
        d_scores = jnp.where(allowed, weights * (d_weights - inner), 0.0)
        d_scores = (d_scores * HEAD_DIM ** (-0.5)).astype(BF16)
        dq_s[part, :] = unstack(nn(d_scores, k[part]))
        dk_s[part, :] = tn(d_scores, stacked_q)

    dq = dq_s[...].astype(BF16)
    dk = dk_s[...].astype(BF16)
    dv = dv_s[...].astype(BF16)
    narrow_s[:, :C] = tn(normed, dq)
    narrow_s[:, C : 2 * C] = tn(normed, dk)
    narrow_s[:, 2 * C : 3 * C] = tn(normed, dv)
    for t in range(4 * C // LANES):
        tile = narrow_s[:, t * LANES : (t + 1) * LANES]
        totals_ref[t * C : (t + 1) * C, :] = tile.astype(BF16)
    spare = totals_ref.shape[0] - TOTAL_ROWS
    if spare:
        totals_ref[TOTAL_ROWS:, :] = jnp.zeros((spare, LANES), BF16)
    d_normed = (nt(dq, w_q) + nt(dk, w_k) + nt(dv, w_v)).astype(BF16).astype(F32)
    grad_ref[...] = (d_resid.astype(F32) + norm_back(center, inverse, d_normed)).astype(BF16)


def reduce_kernel(
    lon_count,
    lat_count,
    rim_parts,
    chunks,
    totals_ref,
    rim_ref,
    grad_qkv_ref,
    grad_proj_ref,
    grad_up_ref,
    grad_down_ref,
    rim_out_ref,
    core_in,
    lat_in,
    far_in,
    half_s,
    part_s,
    result,
    rim_in,
    narrow_s,
    sends,
    receives,
):
    lon, lat = lax.axis_index("lon"), lax.axis_index("lat")
    core, far, far_count = lax.rem(lon, 2), lon // 2, lon_count // 2
    def across(distance):
        return {"lon": lon, "lat": lax.rem(lat + distance + lat_count, lat_count)}

    def along(distance):
        other = lax.rem(far + distance + far_count, far_count)
        return {"lon": other * 2 + core, "lat": lat}

    twin = {"lon": far * 2 + 1 - core, "lat": lat}
    rim_to, rim_from = neighbours(lon_count, lat_count)
    greeted = [twin] + [across(d) for d in range(1, lat_count)]
    greeted += [along(d) for d in range(1, far_count)] + rim_to + rim_from
    greet(greeted)

    used = []

    def send(source, target, device):
        slot = len(used)
        copy = pltpu.make_async_remote_copy(
            src_ref=source,
            dst_ref=target,
            send_sem=sends.at[slot],
            recv_sem=receives.at[slot],
            device_id=device,
            device_id_type=pl.DeviceIdType.MESH,
        )
        copy.start()
        used.append(copy)
        return copy

    def sum_piece(before, chunk):
        part = chunk * far_count
        half = part * lat_count
        part_at, half_at, whole_at = before * far_count, before * far_count * lat_count, 0
        whole_at = 2 * half_at

        def rows(start, index, size):
            return pl.ds(pl.multiple_of(start + index * size, 16), size)

        arriving = core_in.at[pl.ds(half_at, half)]
        first = send(totals_ref.at[rows(whole_at, 1 - core, half)], arriving, twin)
        yield
        first.wait_recv()
        total = totals_ref[rows(whole_at, core, half), :].astype(F32)
        total = total + core_in[pl.ds(half_at, half), :].astype(F32)
        half_s[pl.ds(half_at, half), :] = total.astype(BF16)
        copies = []
        for d in range(1, lat_count):
            source = half_s.at[rows(half_at, lax.rem(lat + d, lat_count), part)]
            copies.append(send(source, lat_in.at[d - 1, pl.ds(part_at, part)], across(d)))
        yield
        total = half_s[rows(half_at, lat, part), :].astype(F32)
        for d, copy in enumerate(copies):
            copy.wait_recv()
            total = total + lat_in[d, pl.ds(part_at, part), :].astype(F32)
        part_s[pl.ds(part_at, part), :] = total.astype(BF16)
        copies = []
        for d in range(1, far_count):
            source = part_s.at[rows(part_at, lax.rem(far + d, far_count), chunk)]
            copies.append(send(source, far_in.at[d - 1, pl.ds(before, chunk)], along(d)))
        yield
        total = part_s[rows(part_at, far, chunk), :].astype(F32)
        for d, copy in enumerate(copies):
            copy.wait_recv()
            total = total + far_in[d, pl.ds(before, chunk), :].astype(F32)
        mine = rows(whole_at, (core * lat_count + lat) * far_count + far, chunk)
        result[mine, :] = total.astype(BF16)
        copies = [send(result.at[mine], result.at[mine], along(d)) for d in range(1, far_count)]
        yield
        for copy in copies:
            copy.wait_recv()
        mine = rows(whole_at, core * lat_count + lat, part)
        copies = [send(result.at[mine], result.at[mine], across(d)) for d in range(1, lat_count)]
        yield
        for copy in copies:
            copy.wait_recv()
        mine = rows(whole_at, core, half)
        last = send(result.at[mine], result.at[mine], twin)
        yield
        last.wait_recv()

    pieces = [sum_piece(sum(chunks[:p]), chunk) for p, chunk in enumerate(chunks)]
    for piece in pieces:
        next(piece)
    rims = []
    at = 0
    for length, device in zip(rim_parts, rim_to):
        window = pl.ds(at, length)
        rims.append(send(rim_ref.at[window], rim_in.at[window], device))
        at += length
    for _ in range(5):
        for piece in pieces:
            next(piece)
    for copy in rims:
        copy.wait_recv()
    rim_out_ref[...] = rim_in[...]
    for piece in pieces:
        next(piece, None)

    for t in range(4 * C // LANES):
        narrow_s[:, t * LANES : (t + 1) * LANES] = result[t * C : (t + 1) * C, :].astype(F32)
    grad_qkv_ref[...] = narrow_s[:, : 3 * C].astype(BF16)
    grad_proj_ref[...] = narrow_s[:, 3 * C :].astype(BF16)
    for t in range(FF // LANES):
        grad_up_ref[:, t * LANES : (t + 1) * LANES] = result[UP_AT + t * C : UP_AT + (t + 1) * C, :]
    for t in range(FF // LANES):
        rows = slice(DOWN_AT + t * C, DOWN_AT + (t + 1) * C)
        grad_down_ref[:, t * LANES : (t + 1) * LANES] = result[rows, :]
    for copy in used:
        copy.wait_send()


def merge_patches(final, merge_weight):
    level_count, row_count, col_count, feat_count = final.shape
    grouped = final.reshape(level_count, row_count // 2, 2, col_count // 2, 2, feat_count)
    grouped = grouped.transpose(0, 1, 3, 2, 4, 5).reshape(-1, 4 * feat_count)
    center, inverse = center_of(grouped.astype(F32))
    merged = nn((center * inverse).astype(BF16), merge_weight).astype(BF16)
    return merged.reshape(level_count, row_count // 2, col_count // 2, 2 * feat_count)


def packed(cuts):
    flat = [cut.reshape(-1, cut.shape[-1]) for cut in cuts]
    lengths = [-(-cut.shape[0] // 16) * 16 for cut in flat]
    padded = [jnp.pad(cut, ((0, n - cut.shape[0]), (0, 0))) for cut, n in zip(flat, lengths)]

    def unpack(buffer):
        starts = [sum(lengths[:i]) for i in range(len(cuts))]
        return [
            buffer[at : at + part.shape[0]].reshape(cut.shape)
            for at, part, cut in zip(starts, flat, cuts)
        ]

    return jnp.concatenate(padded, axis=0), lengths, unpack


def per_device(
    tokens,
    cotangent,
    qkv_codes,
    proj_codes,
    up_codes,
    down_codes,
    bit_widths,
    quant_scales,
    bias_table,
    bias_index,
    merge_weight,
):
    level_count, row_count, col_count, feat_count = tokens.shape
    token_count = level_count * row_count * col_count
    window_rows = row_count // WLAT
    grid_shape = (level_count, row_count, col_count)
    lat_limit = lax.axis_size("lat") * row_count - LAT_PAD
    lat_index = lax.axis_index("lat")
    lat_start = lat_index * row_count - WLAT // 2
    row_ids = lat_index * row_count + jnp.arange(row_count, dtype=jnp.int32)
    row_mask = (row_ids < lat_limit)[None, :, None, None]

    both = jnp.concatenate([tokens, cotangent], axis=-1)
    both = jnp.where(row_mask, both, jnp.zeros_like(both))
    lon_count, lat_count = lax.axis_size("lon"), lax.axis_size("lat")
    rim_rows, rim_cols = WLAT // 2, WLON // 2
    pulled, lengths, unpack = packed(
        [both[:, :-rim_rows, rim_cols:], both[:, -rim_rows:, :rim_cols], both[:, -rim_rows:, rim_cols:]]
    )
    pair = bias_index.reshape(2, HALF, 2, HALF)
    upper, lower = pair[0, :, 0], pair[1, :, 1]
    cut = LANES // 2
    wide = jnp.concatenate([upper[:, :cut], lower[:, :cut]], axis=1)
    tail = jnp.concatenate([upper[:, cut:], lower[:, cut:]], axis=1).reshape(-1, LANES)
    index = jnp.concatenate([wide, tail], axis=0)
    tiles = HALF // (STEPS - 1)
    index = jnp.pad(index, ((0, STEPS * tiles - index.shape[0]), (0, 0)))
    index = index.reshape(STEPS, tiles * LANES)
    positions = bias_table.shape[-1]
    table_rows = window_rows * HEADS
    pieces, piece_rows = -(-positions // PIECE), -(-table_rows // 16) * 16
    table = bias_table.reshape(table_rows, positions)
    spare = ((0, piece_rows - table_rows), (0, pieces * PIECE - positions))
    table = jnp.pad(table, spare).reshape(piece_rows, pieces, PIECE).transpose(1, 0, 2)
    vmem = pl.BlockSpec(memory_space=pltpu.VMEM)
    smem = pl.BlockSpec(memory_space=pltpu.SMEM)
    pulled, bias = pl.pallas_call(
        functools.partial(pull_kernel, lon_count, lat_count, lengths),
        out_shape=[
            jax.ShapeDtypeStruct(pulled.shape, BF16),
            jax.ShapeDtypeStruct((table_rows, WTOK, LANES), F32),
        ],
        in_specs=[vmem] * 3,
        out_specs=[vmem] * 2,
        scratch_shapes=[
            pltpu.VMEM(pulled.shape, BF16),
            pltpu.SemaphoreType.DMA((len(lengths),)),
            pltpu.SemaphoreType.DMA((len(lengths),)),
        ],
        compiler_params=pltpu.CompilerParams(
            collective_id=1, has_side_effects=True, vmem_limit_bytes=32 * 2**20
        ),
        cost_estimate=pl.CostEstimate(
            flops=2 * table.size * index.size, bytes_accessed=20 * 10**6, transcendentals=0
        ),
        name="pull_and_bias",
    )(pulled, index, table)
    got = unpack(pulled)
    upper = jnp.concatenate([got[2], got[1]], axis=2)
    lower = jnp.concatenate([got[0], both[:, :-rim_rows, :rim_cols]], axis=2)
    frame = jnp.concatenate([upper, lower], axis=1).reshape(token_count, 2 * feat_count)

    first_row = lat_start + WLAT * jnp.arange(window_rows, dtype=jnp.int32)
    edges = jnp.stack([-first_row * WLON, (lat_limit - first_row) * WLON], axis=1).reshape(-1)
    operands = (qkv_codes, bias, proj_codes, up_codes, down_codes.T)
    wide = jax.ShapeDtypeStruct((token_count, feat_count), BF16)
    chunk = -(-TOTAL_ROWS // (lon_count * lat_count * 16)) * 16
    total_rows = chunk * lon_count * lat_count
    final, grad, totals = pl.pallas_call(
        functools.partial(block_kernel, window_rows),
        out_shape=[wide, wide, jax.ShapeDtypeStruct((total_rows, LANES), BF16)],
        in_specs=[smem] + [vmem] * 7,
        out_specs=[vmem] * 3,
        scratch_shapes=[pltpu.VMEM((token_count, feat_count), F32)] * 4
        + [pltpu.VMEM((C, 4 * C), F32)],
        compiler_params=pltpu.CompilerParams(vmem_limit_bytes=32 * 2**20),
        cost_estimate=pl.CostEstimate(
            flops=2 * 10**9, bytes_accessed=20 * 10**6, transcendentals=10**6
        ),
        name="block",
    )(
        jnp.concatenate([bit_widths, quant_scales, edges]),
        frame[:, :feat_count],
        frame[:, feat_count:],
        *operands,
    )
    frame = jnp.concatenate([final, grad], axis=-1).reshape(grid_shape + (-1,))
    rim, lengths, unpack = packed(
        [frame[:, rim_rows:, :rim_cols], frame[:, :rim_rows, rim_cols:], frame[:, :rim_rows, :rim_cols]]
    )
    units = chunk // 16
    chunks = [16 * n for n in (units - units // 2, units // 2) if n]
    copies = 2 * (1 + lat_count - 1 + lon_count // 2 - 1) * len(chunks) + len(lengths)
    half = total_rows // 2
    part = half // lat_count
    *grads, rim = pl.pallas_call(
        functools.partial(reduce_kernel, lon_count, lat_count, lengths, chunks),
        out_shape=[
            jax.ShapeDtypeStruct((C, 3 * C), BF16),
            jax.ShapeDtypeStruct((C, C), BF16),
            jax.ShapeDtypeStruct((C, FF), BF16),
            jax.ShapeDtypeStruct((C, FF), BF16),
            jax.ShapeDtypeStruct(rim.shape, BF16),
        ],
        in_specs=[vmem] * 2,
        out_specs=[vmem] * 5,
        scratch_shapes=[
            pltpu.VMEM((half, LANES), BF16),
            pltpu.VMEM((lat_count - 1, part, LANES), BF16),
            pltpu.VMEM((lon_count // 2 - 1, chunk, LANES), BF16),
            pltpu.VMEM((half, LANES), BF16),
            pltpu.VMEM((part, LANES), BF16),
            pltpu.VMEM((total_rows, LANES), BF16),
            pltpu.VMEM(rim.shape, BF16),
            pltpu.VMEM((C, 4 * C), F32),
            pltpu.SemaphoreType.DMA((copies,)),
            pltpu.SemaphoreType.DMA((copies,)),
        ],
        compiler_params=pltpu.CompilerParams(
            collective_id=0, has_side_effects=True, vmem_limit_bytes=48 * 2**20
        ),
        cost_estimate=pl.CostEstimate(
            flops=10**7, bytes_accessed=60 * 10**6, transcendentals=0
        ),
        name="reduce_and_push",
    )(totals, rim)
    got = unpack(rim)
    upper = jnp.concatenate([frame[:, rim_rows:, rim_cols:], got[0]], axis=2)
    lower = jnp.concatenate([got[1], got[2]], axis=2)
    owned = jnp.concatenate([upper, lower], axis=1)
    owned = jnp.where(row_mask, owned, jnp.zeros_like(owned))
    merged = merge_patches(owned[..., :feat_count], merge_weight)
    return (merged, owned[..., feat_count:]) + tuple(grads[:3]) + (grads[3].T,)


def solution(mesh):
    split = P(None, "lat", "lon", None)
    placed = (split, split, P(), P(), P(), P(), P(), P(), P("lat", None, None, None), P(), P())
    return jax.shard_map(
        per_device,
        mesh=mesh,
        in_specs=placed,
        out_specs=(split, split, P(), P(), P(), P()),
        check_vma=False,
    )
```

```python
import functools
import math

import jax
import jax.numpy as jnp
from jax import lax
from jax.experimental import pallas as pl
from jax.experimental.pallas import tpu as pltpu
from jax.sharding import PartitionSpec as P

C = 192
HEADS = 6
FF = 768
HEAD_DIM = 32
WLAT = 6
WLON = 12
LAT_PAD = 11
WTOK = 144
HALF = 72
LANES = 128
PIECE = 256
STEPS = 12
EPSILON = 1e-05
MASKED = -1000000000.0
UP_AT = 6 * C
DOWN_AT = 12 * C
TOTAL_ROWS = 18 * C
F32 = jnp.float32
BF16 = jnp.bfloat16


def nn(left, right):
    return lax.dot_general(left, right, (((1,), (0,)), ((), ())), preferred_element_type=F32)


def nt(left, right):
    return lax.dot_general(left, right, (((1,), (1,)), ((), ())), preferred_element_type=F32)


def tn(left, right):
    return lax.dot_general(left, right, (((0,), (0,)), ((), ())), preferred_element_type=F32)


def neighbours(lon_count, lat_count):
    lon, lat = lax.axis_index("lon"), lax.axis_index("lat")
    west, east = lax.rem(lon + lon_count - 1, lon_count), lax.rem(lon + 1, lon_count)
    north, south = lax.rem(lat + lat_count - 1, lat_count), lax.rem(lat + 1, lat_count)
    behind = [{"lon": west, "lat": lat}, {"lon": lon, "lat": north}, {"lon": west, "lat": north}]
    ahead = [{"lon": east, "lat": lat}, {"lon": lon, "lat": south}, {"lon": east, "lat": south}]
    return behind, ahead


def greet(devices):
    barrier = pltpu.get_barrier_semaphore()
    for device in devices:
        pl.semaphore_signal(barrier, inc=1, device_id=device, device_id_type=pl.DeviceIdType.MESH)
    pl.semaphore_wait(barrier, len(devices))


def pull_kernel(
    lon_count,
    lat_count,
    rim_parts,
    rim_ref,
    index_ref,
    table_ref,
    rim_out_ref,
    bias_ref,
    rim_in,
    sends,
    receives,
):
    behind, ahead = neighbours(lon_count, lat_count)
    greet(behind + ahead)
    copies = []
    at = 0
    for slot, (length, device) in enumerate(zip(rim_parts, ahead)):
        copy = pltpu.make_async_remote_copy(
            src_ref=rim_ref.at[pl.ds(at, length)],
            dst_ref=rim_in.at[pl.ds(at, length)],
            send_sem=sends.at[slot],
            recv_sem=receives.at[slot],
            device_id=device,
            device_id_type=pl.DeviceIdType.MESH,
        )
        copy.start()
        copies.append(copy)
        at += length

    steps, width = index_ref.shape
    table_rows = bias_ref.shape[0]
    pieces, piece_rows, piece = table_ref.shape
    tables = table_ref[...].reshape(pieces * piece_rows, piece)
    inside = lax.broadcasted_iota(jnp.int32, (piece, width), 0)

    def one_step(step, carry):
        index = index_ref[pl.ds(step, 1), :]
        low = jnp.bitwise_and(index, piece - 1)
        high = jnp.right_shift(index, piece.bit_length() - 1)
        chosen = jnp.where(inside == low, 1.0, 0.0).astype(BF16)
        found = nn(tables, chosen)
        total = found[:piece_rows]
        for p in range(1, pieces):
            total = jnp.where(high == p, found[p * piece_rows : (p + 1) * piece_rows], total)
        for i in range(width // LANES):
            for r in range(table_rows):
                row = total[r : r + 1, i * LANES : (i + 1) * LANES]
                bias_ref[r, pl.ds(step * (width // LANES) + i, 1), :] = row
        return carry

    lax.fori_loop(0, steps, one_step, 0)
    for copy in copies:
        copy.wait_recv()
    rim_out_ref[...] = rim_in[...]
    for copy in copies:
        copy.wait_send()


def center_of(values):
    center = values - jnp.mean(values, axis=-1, keepdims=True)
    spread = jnp.mean(center * center, axis=-1, keepdims=True)
    return center, lax.rsqrt(spread + EPSILON)


def norm_back(center, scale, upstream):
    inner = jnp.mean(upstream * center, axis=-1, keepdims=True)
    outer = jnp.mean(upstream, axis=-1, keepdims=True)
    return scale * (upstream - outer - center * (scale * scale * inner))


def block_kernel(
    window_rows,
    scalars_ref,
    start_ref,
    d_out_ref,
    qkv_ref,
    bias_ref,
    proj_ref,
    up_ref,
    down_ref,
    final_ref,
    grad_ref,
    totals_ref,
    heads_s,
    dq_s,
    dk_s,
    dv_s,
    narrow_s,
):
    def dequant(codes, layer, fan_in):
        largest = jnp.left_shift(jnp.int32(1), scalars_ref[layer] - 1) - 1
        scale = jnp.full((1, codes.shape[1]), scalars_ref[4 + layer].astype(F32), F32)
        factor = math.sqrt(C / fan_in) / scale
        return (jnp.clip(codes, -largest, largest).astype(F32) * factor).astype(BF16)

    start = start_ref[...].astype(F32)
    center, inverse = center_of(start)
    normed = (center * inverse).astype(BF16)
    w_q = dequant(qkv_ref[:, :C], 0, C)
    w_k = dequant(qkv_ref[:, C : 2 * C], 0, C)
    w_v = dequant(qkv_ref[:, 2 * C :], 0, C)
    q = nn(normed, w_q).astype(BF16)
    k = nn(normed, w_k).astype(BF16)
    v = nn(normed, w_v).astype(BF16)

    lane = lax.broadcasted_iota(jnp.int32, (HALF, C), 1)
    head_masks = [(lane >= h * HEAD_DIM) & (lane < (h + 1) * HEAD_DIM) for h in range(HEADS)]

    def stack(values):
        wide = values.astype(F32)
        return jnp.concatenate([jnp.where(m, wide, 0.0) for m in head_masks], axis=0).astype(BF16)

    def unstack(values):
        total = jnp.zeros((HALF, C), F32)
        for h, m in enumerate(head_masks):
            total = jnp.where(m, values[h * HALF : (h + 1) * HALF], total)
        return total

    keys = lax.broadcasted_iota(jnp.int32, (HEADS * HALF, HALF), 1)
    blocks = start.shape[0] // HALF
    saved = []
    for b in range(blocks):
        level, a = b // window_rows, b % window_rows
        part = slice(b * HALF, (b + 1) * HALF)
        stacked_q = stack(q[part])
        bias = bias_ref[a * HEADS : (a + 1) * HEADS, (1 - level) * HALF : (2 - level) * HALF, :]
        bias = bias.reshape(HEADS * HALF, LANES)[:, :HALF]
        scores = nt(stacked_q, k[part]) * HEAD_DIM ** (-0.5) + bias
        allowed = (keys >= scalars_ref[8 + 2 * a]) & (keys < scalars_ref[9 + 2 * a])
        scores = jnp.where(allowed, scores, MASKED)
        weights = jnp.exp(scores - jnp.max(scores, axis=-1, keepdims=True))
        weights = weights / jnp.sum(weights, axis=-1, keepdims=True)
        saved.append((stacked_q, weights, allowed))
        heads_s[part, :] = unstack(nn(weights.astype(BF16), v[part]))

    heads = heads_s[...].astype(BF16)
    w_proj = dequant(proj_ref[...], 1, C)
    resid = (start + nn(heads, w_proj)).astype(BF16)
    center_two, inverse_two = center_of(resid.astype(F32))
    normed_two = (center_two * inverse_two).astype(BF16)
    w_up = dequant(up_ref[...], 2, C)
    w_down_t = dequant(down_ref[...], 3, FF)
    pre = nn(normed_two, w_up)
    cubic = math.sqrt(2 / math.pi)
    square = pre * pre
    bent = jnp.tanh(cubic * (pre + 0.044715 * square * pre))
    hidden = (0.5 * pre * (1.0 + bent)).astype(BF16)
    final_ref[...] = (resid.astype(F32) + nt(hidden, w_down_t)).astype(BF16)
    d_out = d_out_ref[...]
    down_total = tn(d_out, hidden).astype(BF16)
    for t in range(FF // LANES):
        rows = slice(DOWN_AT + t * C, DOWN_AT + (t + 1) * C)
        totals_ref[rows, :] = down_total[:, t * LANES : (t + 1) * LANES]
    d_hidden = nn(d_out, w_down_t).astype(BF16).astype(F32)
    slope = 0.5 * (1.0 + bent) + 0.5 * pre * (1.0 - bent * bent) * cubic * (
        1.0 + 3 * 0.044715 * square
    )
    d_pre = (slope * d_hidden).astype(BF16)
    up_total = tn(normed_two, d_pre).astype(BF16)
    for t in range(FF // LANES):
        totals_ref[UP_AT + t * C : UP_AT + (t + 1) * C, :] = up_total[:, t * LANES : (t + 1) * LANES]
    d_normed_two = nt(d_pre, w_up).astype(BF16).astype(F32)
    d_resid = (d_out.astype(F32) + norm_back(center_two, inverse_two, d_normed_two)).astype(BF16)
    narrow_s[:, 3 * C :] = tn(heads, d_resid)
    d_heads = nt(d_resid, w_proj).astype(BF16)

    for b in range(blocks):
        part = slice(b * HALF, (b + 1) * HALF)
        stacked_q, weights, allowed = saved[b]
        d_stacked = stack(d_heads[part])
        d_weights = nt(d_stacked, v[part]).astype(BF16).astype(F32)
        dv_s[part, :] = tn(weights.astype(BF16), d_stacked)
        inner = jnp.sum(weights * d_weights, axis=-1, keepdims=True)
        d_scores = jnp.where(allowed, weights * (d_weights - inner), 0.0)
        d_scores = (d_scores * HEAD_DIM ** (-0.5)).astype(BF16)
        dq_s[part, :] = unstack(nn(d_scores, k[part]))
        dk_s[part, :] = tn(d_scores, stacked_q)

    dq = dq_s[...].astype(BF16)
    dk = dk_s[...].astype(BF16)
    dv = dv_s[...].astype(BF16)
    narrow_s[:, :C] = tn(normed, dq)
    narrow_s[:, C : 2 * C] = tn(normed, dk)
    narrow_s[:, 2 * C : 3 * C] = tn(normed, dv)
    for t in range(4 * C // LANES):
        tile = narrow_s[:, t * LANES : (t + 1) * LANES]
        totals_ref[t * C : (t + 1) * C, :] = tile.astype(BF16)
    spare = totals_ref.shape[0] - TOTAL_ROWS
    if spare:
        totals_ref[TOTAL_ROWS:, :] = jnp.zeros((spare, LANES), BF16)
    d_normed = (nt(dq, w_q) + nt(dk, w_k) + nt(dv, w_v)).astype(BF16).astype(F32)
    grad_ref[...] = (d_resid.astype(F32) + norm_back(center, inverse, d_normed)).astype(BF16)


def reduce_kernel(
    lon_count,
    lat_count,
    rim_parts,
    chunks,
    totals_ref,
    rim_ref,
    grad_qkv_ref,
    grad_proj_ref,
    grad_up_ref,
    grad_down_ref,
    rim_out_ref,
    core_in,
    lat_in,
    far_in,
    half_s,
    part_s,
    result,
    rim_in,
    narrow_s,
    sends,
    receives,
):
    lon, lat = lax.axis_index("lon"), lax.axis_index("lat")
    core, far, far_count = lax.rem(lon, 2), lon // 2, lon_count // 2
    def across(distance):
        return {"lon": lon, "lat": lax.rem(lat + distance + lat_count, lat_count)}

    def along(distance):
        other = lax.rem(far + distance + far_count, far_count)
        return {"lon": other * 2 + core, "lat": lat}

    twin = {"lon": far * 2 + 1 - core, "lat": lat}
    rim_to, rim_from = neighbours(lon_count, lat_count)
    greeted = [twin] + [across(d) for d in range(1, lat_count)]
    greeted += [along(d) for d in range(1, far_count)] + rim_to + rim_from
    greet(greeted)

    used = []

    def send(source, target, device):
        slot = len(used)
        copy = pltpu.make_async_remote_copy(
            src_ref=source,
            dst_ref=target,
            send_sem=sends.at[slot],
            recv_sem=receives.at[slot],
            device_id=device,
            device_id_type=pl.DeviceIdType.MESH,
        )
        copy.start()
        used.append(copy)
        return copy

    def sum_piece(before, chunk):
        part = chunk * far_count
        half = part * lat_count
        part_at, half_at, whole_at = before * far_count, before * far_count * lat_count, 0
        whole_at = 2 * half_at

        def rows(start, index, size):
            return pl.ds(pl.multiple_of(start + index * size, 16), size)

        arriving = core_in.at[pl.ds(half_at, half)]
        first = send(totals_ref.at[rows(whole_at, 1 - core, half)], arriving, twin)
        yield
        first.wait_recv()
        total = totals_ref[rows(whole_at, core, half), :].astype(F32)
        total = total + core_in[pl.ds(half_at, half), :].astype(F32)
        half_s[pl.ds(half_at, half), :] = total.astype(BF16)
        copies = []
        for d in range(1, lat_count):
            source = half_s.at[rows(half_at, lax.rem(lat + d, lat_count), part)]
            copies.append(send(source, lat_in.at[d - 1, pl.ds(part_at, part)], across(d)))
        yield
        total = half_s[rows(half_at, lat, part), :].astype(F32)
        for d, copy in enumerate(copies):
            copy.wait_recv()
            total = total + lat_in[d, pl.ds(part_at, part), :].astype(F32)
        part_s[pl.ds(part_at, part), :] = total.astype(BF16)
        copies = []
        for d in range(1, far_count):
            source = part_s.at[rows(part_at, lax.rem(far + d, far_count), chunk)]
            copies.append(send(source, far_in.at[d - 1, pl.ds(before, chunk)], along(d)))
        yield
        total = part_s[rows(part_at, far, chunk), :].astype(F32)
        for d, copy in enumerate(copies):
            copy.wait_recv()
            total = total + far_in[d, pl.ds(before, chunk), :].astype(F32)
        mine = rows(whole_at, (core * lat_count + lat) * far_count + far, chunk)
        result[mine, :] = total.astype(BF16)
        copies = [send(result.at[mine], result.at[mine], along(d)) for d in range(1, far_count)]
        yield
        for copy in copies:
            copy.wait_recv()
        mine = rows(whole_at, core * lat_count + lat, part)
        copies = [send(result.at[mine], result.at[mine], across(d)) for d in range(1, lat_count)]
        yield
        for copy in copies:
            copy.wait_recv()
        mine = rows(whole_at, core, half)
        last = send(result.at[mine], result.at[mine], twin)
        yield
        last.wait_recv()

    pieces = [sum_piece(sum(chunks[:p]), chunk) for p, chunk in enumerate(chunks)]
    for piece in pieces:
        next(piece)
    rims = []
    at = 0
    for length, device in zip(rim_parts, rim_to):
        window = pl.ds(at, length)
        rims.append(send(rim_ref.at[window], rim_in.at[window], device))
        at += length
    for _ in range(5):
        for piece in pieces:
            next(piece)
    for copy in rims:
        copy.wait_recv()
    rim_out_ref[...] = rim_in[...]
    for piece in pieces:
        next(piece, None)

    for t in range(4 * C // LANES):
        narrow_s[:, t * LANES : (t + 1) * LANES] = result[t * C : (t + 1) * C, :].astype(F32)
    grad_qkv_ref[...] = narrow_s[:, : 3 * C].astype(BF16)
    grad_proj_ref[...] = narrow_s[:, 3 * C :].astype(BF16)
    for t in range(FF // LANES):
        grad_up_ref[:, t * LANES : (t + 1) * LANES] = result[UP_AT + t * C : UP_AT + (t + 1) * C, :]
    for t in range(FF // LANES):
        rows = slice(DOWN_AT + t * C, DOWN_AT + (t + 1) * C)
        grad_down_ref[:, t * LANES : (t + 1) * LANES] = result[rows, :]
    for copy in used:
        copy.wait_send()


def merge_patches(final, merge_weight):
    level_count, row_count, col_count, feat_count = final.shape
    grouped = final.reshape(level_count, row_count // 2, 2, col_count // 2, 2, feat_count)
    grouped = grouped.transpose(0, 1, 3, 2, 4, 5).reshape(-1, 4 * feat_count)
    center, inverse = center_of(grouped.astype(F32))
    merged = nn((center * inverse).astype(BF16), merge_weight).astype(BF16)
    return merged.reshape(level_count, row_count // 2, col_count // 2, 2 * feat_count)


def packed(cuts):
    flat = [cut.reshape(-1, cut.shape[-1]) for cut in cuts]
    lengths = [-(-cut.shape[0] // 16) * 16 for cut in flat]
    padded = [jnp.pad(cut, ((0, n - cut.shape[0]), (0, 0))) for cut, n in zip(flat, lengths)]

    def unpack(buffer):
        starts = [sum(lengths[:i]) for i in range(len(cuts))]
        return [
            buffer[at : at + part.shape[0]].reshape(cut.shape)
            for at, part, cut in zip(starts, flat, cuts)
        ]

    return jnp.concatenate(padded, axis=0), lengths, unpack


def per_device(
    tokens,
    cotangent,
    qkv_codes,
    proj_codes,
    up_codes,
    down_codes,
    bit_widths,
    quant_scales,
    bias_table,
    bias_index,
    merge_weight,
):
    level_count, row_count, col_count, feat_count = tokens.shape
    token_count = level_count * row_count * col_count
    window_rows = row_count // WLAT
    grid_shape = (level_count, row_count, col_count)
    lat_limit = lax.axis_size("lat") * row_count - LAT_PAD
    lat_index = lax.axis_index("lat")
    lat_start = lat_index * row_count - WLAT // 2
    row_ids = lat_index * row_count + jnp.arange(row_count, dtype=jnp.int32)
    row_mask = (row_ids < lat_limit)[None, :, None, None]

    both = jnp.concatenate([tokens, cotangent], axis=-1)
    both = jnp.where(row_mask, both, jnp.zeros_like(both))
    lon_count, lat_count = lax.axis_size("lon"), lax.axis_size("lat")
    rim_rows, rim_cols = WLAT // 2, WLON // 2
    pulled, lengths, unpack = packed(
        [both[:, :-rim_rows, rim_cols:], both[:, -rim_rows:, :rim_cols], both[:, -rim_rows:, rim_cols:]]
    )
    pair = bias_index.reshape(2, HALF, 2, HALF)
    index = jnp.concatenate([pair[0, :, 0], pair[1, :, 1]], axis=0)
    index = jnp.pad(index, ((0, 0), (0, LANES - HALF))).reshape(STEPS, -1)
    positions = bias_table.shape[-1]
    table_rows = window_rows * HEADS
    pieces, piece_rows = -(-positions // PIECE), -(-table_rows // 16) * 16
    table = bias_table.reshape(table_rows, positions)
    spare = ((0, piece_rows - table_rows), (0, pieces * PIECE - positions))
    table = jnp.pad(table, spare).reshape(piece_rows, pieces, PIECE).transpose(1, 0, 2)
    vmem = pl.BlockSpec(memory_space=pltpu.VMEM)
    smem = pl.BlockSpec(memory_space=pltpu.SMEM)
    pulled, bias = pl.pallas_call(
        functools.partial(pull_kernel, lon_count, lat_count, lengths),
        out_shape=[
            jax.ShapeDtypeStruct(pulled.shape, BF16),
            jax.ShapeDtypeStruct((table_rows, WTOK, LANES), F32),
        ],
        in_specs=[vmem] * 3,
        out_specs=[vmem] * 2,
        scratch_shapes=[
            pltpu.VMEM(pulled.shape, BF16),
            pltpu.SemaphoreType.DMA((len(lengths),)),
            pltpu.SemaphoreType.DMA((len(lengths),)),
        ],
        compiler_params=pltpu.CompilerParams(
            collective_id=1, has_side_effects=True, vmem_limit_bytes=32 * 2**20
        ),
        cost_estimate=pl.CostEstimate(
            flops=2 * table.size * index.size, bytes_accessed=20 * 10**6, transcendentals=0
        ),
        name="pull_and_bias",
    )(pulled, index, table)
    got = unpack(pulled)
    upper = jnp.concatenate([got[2], got[1]], axis=2)
    lower = jnp.concatenate([got[0], both[:, :-rim_rows, :rim_cols]], axis=2)
    frame = jnp.concatenate([upper, lower], axis=1).reshape(token_count, 2 * feat_count)

    first_row = lat_start + WLAT * jnp.arange(window_rows, dtype=jnp.int32)
    edges = jnp.stack([-first_row * WLON, (lat_limit - first_row) * WLON], axis=1).reshape(-1)
    operands = (qkv_codes, bias, proj_codes, up_codes, down_codes.T)
    wide = jax.ShapeDtypeStruct((token_count, feat_count), BF16)
    chunk = -(-TOTAL_ROWS // (lon_count * lat_count * 16)) * 16
    total_rows = chunk * lon_count * lat_count
    final, grad, totals = pl.pallas_call(
        functools.partial(block_kernel, window_rows),
        out_shape=[wide, wide, jax.ShapeDtypeStruct((total_rows, LANES), BF16)],
        in_specs=[smem] + [vmem] * 7,
        out_specs=[vmem] * 3,
        scratch_shapes=[pltpu.VMEM((token_count, feat_count), F32)] * 4
        + [pltpu.VMEM((C, 4 * C), F32)],
        compiler_params=pltpu.CompilerParams(vmem_limit_bytes=32 * 2**20),
        cost_estimate=pl.CostEstimate(
            flops=2 * 10**9, bytes_accessed=20 * 10**6, transcendentals=10**6
        ),
        name="block",
    )(
        jnp.concatenate([bit_widths, quant_scales, edges]),
        frame[:, :feat_count],
        frame[:, feat_count:],
        *operands,
    )
    frame = jnp.concatenate([final, grad], axis=-1).reshape(grid_shape + (-1,))
    rim, lengths, unpack = packed(
        [frame[:, rim_rows:, :rim_cols], frame[:, :rim_rows, rim_cols:], frame[:, :rim_rows, :rim_cols]]
    )
    units = chunk // 16
    chunks = [16 * n for n in ((units + 2) // 3, (units + 1) // 3, units // 3) if n]
    copies = 2 * (1 + lat_count - 1 + lon_count // 2 - 1) * len(chunks) + len(lengths)
    half = total_rows // 2
    part = half // lat_count
    *grads, rim = pl.pallas_call(
        functools.partial(reduce_kernel, lon_count, lat_count, lengths, chunks),
        out_shape=[
            jax.ShapeDtypeStruct((C, 3 * C), BF16),
            jax.ShapeDtypeStruct((C, C), BF16),
            jax.ShapeDtypeStruct((C, FF), BF16),
            jax.ShapeDtypeStruct((C, FF), BF16),
            jax.ShapeDtypeStruct(rim.shape, BF16),
        ],
        in_specs=[vmem] * 2,
        out_specs=[vmem] * 5,
        scratch_shapes=[
            pltpu.VMEM((half, LANES), BF16),
            pltpu.VMEM((lat_count - 1, part, LANES), BF16),
            pltpu.VMEM((lon_count // 2 - 1, chunk, LANES), BF16),
            pltpu.VMEM((half, LANES), BF16),
            pltpu.VMEM((part, LANES), BF16),
            pltpu.VMEM((total_rows, LANES), BF16),
            pltpu.VMEM(rim.shape, BF16),
            pltpu.VMEM((C, 4 * C), F32),
            pltpu.SemaphoreType.DMA((copies,)),
            pltpu.SemaphoreType.DMA((copies,)),
        ],
        compiler_params=pltpu.CompilerParams(
            collective_id=0, has_side_effects=True, vmem_limit_bytes=48 * 2**20
        ),
        cost_estimate=pl.CostEstimate(
            flops=10**7, bytes_accessed=60 * 10**6, transcendentals=0
        ),
        name="reduce_and_push",
    )(totals, rim)
    got = unpack(rim)
    upper = jnp.concatenate([frame[:, rim_rows:, rim_cols:], got[0]], axis=2)
    lower = jnp.concatenate([got[1], got[2]], axis=2)
    owned = jnp.concatenate([upper, lower], axis=1)
    owned = jnp.where(row_mask, owned, jnp.zeros_like(owned))
    merged = merge_patches(owned[..., :feat_count], merge_weight)
    return (merged, owned[..., feat_count:]) + tuple(grads[:3]) + (grads[3].T,)


def solution(mesh):
    split = P(None, "lat", "lon", None)
    placed = (split, split, P(), P(), P(), P(), P(), P(), P("lat", None, None, None), P(), P())
    return jax.shard_map(
        per_device,
        mesh=mesh,
        in_specs=placed,
        out_specs=(split, split, P(), P(), P(), P()),
        check_vma=False,
    )
```
